512 devices in a mesh: leaf: 128 (over y, z, core), rhs: 4 (over x).
Axes of the slice: x: 4, y: 4, z: 16, core: 2. Of those that a mesh axis runs over, the one named last changes fastest.
Arguments:
- coeffs: bfloat16 [64, 32768], P('rhs', 'leaf'), may hold values from -6 to 6
- near_blocks: bfloat16 [5120, 128, 128], P('leaf'), may hold values from -0.125 to 0.125
- near_scale: int32 [5120], P('leaf'), may hold values from -1 to 1
- near_target: int32 [5120], replicated, may hold values from 0 to 255, as said below
- near_source: int32 [5120], replicated, may hold values from 0 to 255, as said below
- src_basis: bfloat16 [256, 32, 128], P('leaf'), may hold values from -0.5 to 0.5
- tgt_basis: bfloat16 [256, 32, 128], P('leaf'), may hold values from -1 to 1
- couplings: bfloat16 [4096, 32, 32], P(('leaf', 'rhs')), may hold values from -0.25 to 0.25
- far_target: int32 [4096], replicated, may hold values from 0 to 255, as said below
- far_source: int32 [4096], replicated, may hold values from 0 to 255, as said below
Outputs:
- potentials: float32 [64, 32768], P('rhs', 'leaf')
The draws below stay inside these ranges and needn't reach their ends.
Inputs may be any that keep to these rules, and one draw needn't show every extreme that they name: `near_source`: block b is held by leaf device b // 40; cluster c lies on leaf device c // 2. Of one holder's blocks at most 2 have their source cluster on one leaf device, and for every holder some leaf device supplies exactly 2. `near_target`: of one holder's blocks at most 2 have their target cluster on one leaf device, and for every holder some leaf device receives exactly 2. (Blocks are dealt to holders for load balance, independently of their block rows.). `far_source`: pair q's source cluster lies on leaf device q // 32. `far_target`: of the pairs whose sources lie on one leaf device, at most 2 have their target cluster on one leaf device, and for every such device some leaf device receives exactly 2.
All inputs are finite; a program needn't handle non-finite values.
Results may differ from the reference program's by a relative error of at most 0.0026.
Values may be sent and summed in bfloat16 or wider, within the bound.
A program may use at most 64 MiB of HBM per device.

```python
import jax
import jax.numpy as jnp
from jax import lax

CLUSTER = 128
NRHS = 64
RANK = 32
NEAR_ROW = 20
FAR_ROW = 16
CL_DEV = 2
NCL = 256
PANELS = 32768
BLK_DEV = 40
NBLK = 5120
CAP = 2
FAR_LEAF = 32
NFAR = 4096
FCAP = 2


def spread_devices(key, count, cap, groups):
    key_order, key_rest, key_mix = jax.random.split(key, 3)
    order = jax.random.permutation(key_order, groups).astype(jnp.int32)
    others = jax.random.permutation(key_rest, jnp.repeat(order[1:], cap))
    seq = jnp.concatenate([jnp.full((cap,), order[0], jnp.int32), others.astype(jnp.int32)])[:count]
    return jax.random.permutation(key_mix, seq)


def clusters_for(key, count, cap):
    groups = NCL // CL_DEV
    keys = jax.random.split(key, groups)

    def one_holder(holder_key):
        key_dev, key_local = jax.random.split(holder_key)
        devices = spread_devices(key_dev, count, cap, groups)
        return devices * CL_DEV + jax.random.randint(key_local, (count,), 0, CL_DEV).astype(jnp.int32)
    return jax.vmap(one_holder)(keys).reshape(-1).astype(jnp.int32)


def draw_near_source(key, part):
    key = jax.random.fold_in(key, 11)
    return clusters_for(key, BLK_DEV, CAP)


def draw_near_target(key, part):
    key = jax.random.fold_in(key, 12)
    return clusters_for(key, BLK_DEV, CAP)


def draw_far_target(key, part):
    key = jax.random.fold_in(key, 13)
    return clusters_for(key, FAR_LEAF, FCAP)


def draw_far_source(key, part):
    key = jax.random.fold_in(key, 14)
    groups = NCL // CL_DEV
    owners = jnp.repeat(jnp.arange(groups, dtype=jnp.int32), FAR_LEAF)
    local = jax.random.randint(key, (NFAR,), 0, CL_DEV).astype(jnp.int32)
    return owners * CL_DEV + local


def with_ends(result, rng, low, top_value):
    spot = [jax.random.randint(jax.random.fold_in(rng, axis), (), 0, length) for axis, length in enumerate(result.shape)]
    longest = result.shape.index(max(result.shape))
    neighbour = spot[:longest] + [(spot[longest] + 1) % result.shape[longest]] + spot[longest + 1:]
    return result.at[tuple(spot)].set(low).at[tuple(neighbour)].set(top_value)


def steps_of(rng, shape, cuts, least, high):
    loudness, own = 1.0, jax.random.fold_in(rng, 6)
    for dim, blocks in cuts:
        steps = jnp.exp(jax.random.uniform(jax.random.fold_in(own, dim), (blocks,), jnp.float32, least / len(cuts), high / len(cuts)))
        loudness = loudness * jnp.repeat(steps, shape[dim] // blocks).reshape([-1 if axis == dim else 1 for axis in range(len(shape))])
    return loudness


def centred(stream_key, extent, scale, most, cuts=(), kind=jnp.bfloat16):
    array = scale * jax.random.normal(stream_key, extent, jnp.float32)
    if cuts:
        array = array * steps_of(stream_key, extent, cuts, -0.22, 0.18)
    return jnp.clip(array, -most, most).astype(kind)


def setup_inputs(seed: int = 0) -> dict:
    key_of = jax.random.split(jax.random.key(seed), 11)
    coeffs = centred(key_of[0], (NRHS, PANELS), 1.0, 6.0, ((0, 4), (1, 128)))
    near_blocks = centred(key_of[1], (NBLK, CLUSTER, CLUSTER), (CLUSTER * NEAR_ROW) ** -0.5, 0.125, ((0, 128),))
    near_scale = with_ends(jax.random.randint(key_of[2], (NBLK,), -1, 2), jax.random.fold_in(key_of[2], 1), -1, 1).astype(jnp.int32)
    near_target = draw_near_target(jax.random.fold_in(key_of[10], 71), 0)
    near_source = draw_near_source(jax.random.fold_in(key_of[10], 71), 0)
    src_basis = centred(key_of[5], (NCL, RANK, CLUSTER), CLUSTER ** -0.5, 0.5, ((0, 128),))
    tgt_basis = centred(key_of[6], (NCL, RANK, CLUSTER), RANK ** -0.5, 1.0, ((0, 128),))
    couplings = centred(key_of[7], (NFAR, RANK, RANK), (RANK * FAR_ROW) ** -0.5, 0.25, ((0, 512),))
    far_target = draw_far_target(jax.random.fold_in(key_of[10], 71), 0)
    far_source = draw_far_source(jax.random.fold_in(key_of[10], 71), 0)
    return {"coeffs": coeffs, "near_blocks": near_blocks, "near_scale": near_scale, "near_target": near_target, "near_source": near_source, "src_basis": src_basis, "tgt_basis": tgt_basis, "couplings": couplings, "far_target": far_target, "far_source": far_source}


def reference(coeffs, near_blocks, near_scale, near_target, near_source, src_basis, tgt_basis, couplings, far_target, far_source):
    xc = coeffs.reshape(NRHS, NCL, CLUSTER).transpose(1, 0, 2)
    groups = NBLK // BLK_DEV
    blocks_all = near_blocks.reshape(groups, BLK_DEV, CLUSTER, CLUSTER)
    scale_all = near_scale.reshape(groups, BLK_DEV)
    target_all = near_target.reshape(groups, BLK_DEV)
    source_all = near_source.reshape(groups, BLK_DEV)

    def add_group(total, pieces):
        blocks, scales, targets, sources = pieces
        picked = xc[sources].astype(jnp.float32)
        term = jnp.einsum('bfj,bij->bfi', picked, blocks.astype(jnp.float32))
        term = term * jnp.exp2(scales.astype(jnp.float32))[:, None, None]
        return total + jax.ops.segment_sum(term, targets, num_segments=NCL), None

    start = jnp.zeros((NCL, NRHS, CLUSTER), jnp.float32)
    near_sum, unused = lax.scan(add_group, start, (blocks_all, scale_all, target_all, source_all))
    basis_x = jnp.einsum('cfp,crp->cfr', xc.astype(jnp.float32), src_basis.astype(jnp.float32)).astype(jnp.bfloat16)
    far_term = jnp.einsum('qfi,qoi->qfo', basis_x[far_source].astype(jnp.float32), couplings.astype(jnp.float32))
    far_hat = jax.ops.segment_sum(far_term, far_target, num_segments=NCL).astype(jnp.bfloat16)
    far_sum = jnp.einsum('cfr,crp->cfp', far_hat.astype(jnp.float32), tgt_basis.astype(jnp.float32))
    total = near_sum + far_sum
    return total.transpose(1, 0, 2).reshape(NRHS, NCL * CLUSTER)
```

```python
import jax
import jax.numpy as jnp
from jax import lax
from jax.experimental import pallas as pl
from jax.experimental.pallas import tpu as pltpu
from jax.sharding import PartitionSpec as P

MESH = pl.DeviceIdType.MESH
NY, NZ, NX = 4, 16, 4
MID = 8
BLK = 40
CHUNK = 8
NCHUNK = BLK // CHUNK
PAIRS = 32
SHARE = 8
GROUPS = ((4, 9), (0, 4), (13, 3))
Z_ORDER = (8, 7, 9, 6, 10, 5, 11, 4, 12, 3, 13, 2, 14, 1, 15)
F32, BF16 = jnp.float32, jnp.bfloat16
NT = (((1,), (1,)), ((), ()))


def kernel(
    coeffs, blocks, scale, ntgt, nsrc, src_basis, tgt_basis, couplings, ftgt, fsrc,
    out,
    x_in, blk, scale_s, ntgt_v, nsrc_s, sb, tb, coup, ftgt_v, fsrc_s,
    xg, pg, fg, bx, t2n, t2f, v2, kr, kf, acc, fa, zs_buf, zr_buf,
    lsem, zsem, ysem, csem, fsem, psem, rsem,
):
    me = lax.axis_index("leaf")
    x = lax.axis_index("rhs")
    y, z, c = me // 32, (me // 2) % 16, me % 2

    def leaf(yo, zo, co):
        return (((y + yo) % NY) * NZ + (z + zo) % NZ) * 2 + (c + co) % 2

    def at(yo, zo, co):
        return {"leaf": leaf(yo, zo, co)}

    barrier = pltpu.get_barrier_semaphore()
    for zo in Z_ORDER:
        pl.semaphore_signal(barrier, inc=1, device_id=at(0, zo, 0), device_id_type=MESH)
    for yo in (2, 1, 3):
        pl.semaphore_signal(barrier, inc=1, device_id=at(yo, 0, 0), device_id_type=MESH)
    pl.semaphore_signal(barrier, inc=1, device_id=at(0, 0, 1), device_id_type=MESH)
    for xo in range(1, NX):
        pl.semaphore_signal(barrier, inc=1, device_id={"rhs": (x + xo) % NX}, device_id_type=MESH)

    local = []
    pairs = (
        (coeffs, x_in), (src_basis, sb), (ntgt, ntgt_v), (ftgt, ftgt_v),
        (couplings, coup.at[pl.ds(x * SHARE, SHARE)]), (fsrc, fsrc_s), (nsrc, nsrc_s), (scale, scale_s),
        (blocks, blk), (tgt_basis, tb),
    )
    for i, (a, b) in enumerate(pairs):
        copy = pltpu.make_async_copy(a, b, lsem.at[i])
        copy.start()
        local.append(copy)

    started = []

    def send(src, dst, sems, index, device):
        copy = pltpu.make_async_remote_copy(
            src_ref=src, dst_ref=dst, send_sem=sems.at[0, index], recv_sem=sems.at[1, index],
            device_id=device, device_id_type=MESH,
        )
        copy.start()
        started.append(copy)
        return copy

    own = 2 * MID
    local[0].wait()
    xg[own] = x_in[:, 0:128]
    xg[own + 1] = x_in[:, 128:256]
    local[1].wait()
    for k in range(2):
        part = lax.dot_general(xg[own + k], sb[k], NT, preferred_element_type=F32)
        bx[k] = part.astype(BF16)

    local[2].wait()
    local[3].wait()
    lane = lax.broadcasted_iota(jnp.int32, (16, 128), 1)
    sub = lax.broadcasted_iota(jnp.int32, (16, 128), 0)
    near_rows = jnp.zeros((16, 128), jnp.int32)
    far_rows = jnp.zeros((16, 128), jnp.int32)
    for h in range(8):
        leaf_h = leaf(h // 2, 0, h % 2)
        first = leaf_h * BLK
        row, off = first // 128, first % 128
        after = jnp.minimum(row + 1, BLK - 1)
        back = (128 - off) % 128
        one = jnp.broadcast_to(ntgt_v[pl.ds(row, 1), :], (16, 128))
        two = jnp.broadcast_to(ntgt_v[pl.ds(after, 1), :], (16, 128))
        both = pltpu.roll(jnp.where(lane >= off, one, two), back, 1)
        near_rows = jnp.where(sub == h, both, near_rows)
        frow, foff = leaf_h // 4, (leaf_h % 4) * 32
        fone = jnp.broadcast_to(ftgt_v[pl.ds(frow, 1), :], (16, 128))
        far_rows = jnp.where(sub == h, pltpu.roll(fone, (128 - foff) % 128, 1), far_rows)
    near_rows = near_rows.astype(F32).astype(BF16)
    far_rows = far_rows.astype(F32).astype(BF16)

    def spread(rows, width, step, start):
        b = lax.broadcasted_iota(jnp.int32, (128, width), 0)
        l = lax.broadcasted_iota(jnp.int32, (128, width), 1)
        pick = jnp.where(b == (l // 16) * step + start, 1.0, 0.0).astype(BF16)
        f = lax.broadcasted_iota(jnp.int32, (16, width), 1) % 16
        return jnp.dot(rows, pick, preferred_element_type=F32) * 16.0 + f.astype(F32)

    t2n[...] = spread(near_rows, BLK * 16, 1, 0)
    t2f[0] = spread(far_rows, 256, 2, 0)
    t2f[1] = spread(far_rows, 256, 2, 1)
    r = lax.broadcasted_iota(jnp.int32, (512, 128), 0)
    z_dst = (z + r // 32 + (NZ - MID)) % NZ
    v2[...] = ((((y * NZ + z_dst) * 2 + c) * 2 + (r // 16) % 2) * 16 + r % 16).astype(F32)

    local[4].wait()
    pl.semaphore_wait(barrier, 22)

    tile = xg.at[pl.ds(own, 2)]
    z_copies = {}
    for zo in Z_ORDER:
        slot = (MID - zo) % NZ
        z_copies[slot] = send(tile, xg.at[pl.ds(2 * slot, 2)], zsem, slot, at(0, zo, 0))
    mine = coup.at[pl.ds(x * SHARE, SHARE)]
    c_copies = [
        send(mine, mine, csem, xo - 1, {"rhs": (x + xo) % NX}) for xo in range(1, NX)
    ]

    def build(i, carry):
        rows = pl.ds(pl.multiple_of(i * 32, 32), 32)
        want = v2[rows, :]
        for g in range(NCHUNK):
            for h in range(8):
                row = t2n[h : h + 1, g * 128 : (g + 1) * 128]
                kr[rows, (g * 8 + h) * 128 : (g * 8 + h + 1) * 128] = jnp.where(row == want, 1.0, 0.0).astype(BF16)
        for g in range(2):
            for h in range(8):
                for half in range(2):
                    row = t2f[g, h : h + 1, half * 128 : (half + 1) * 128]
                    at_lane = (h * 2 + half) * 128
                    kf[g, rows, at_lane : at_lane + 128] = jnp.where(row == want, 1.0, 0.0).astype(BF16)
        return carry

    lax.fori_loop(0, 16, build, 0)

    def x_span(yo, co, group):
        first, count = GROUPS[group]
        return xg.at[pl.ds(((yo * 2 + co) * NZ + first) * 2, count * 2)]

    y_copies = {}

    def forward(group):
        for yo in (2, 1, 3):
            there = (NY - yo) % NY
            y_copies[there, 0, group] = send(
                x_span(0, 0, group), x_span(there, 0, group), ysem, (there * 2) * 3 + group, at(yo, 0, 0)
            )
        relay(0, group)

    def relay(yo, group):
        y_copies[yo, 1, group] = send(
            x_span(yo, 0, group), x_span(yo, 1, group), ysem, (yo * 2 + 1) * 3 + group, at(0, 0, 1)
        )

    def wait_group(group):
        first, count = GROUPS[group]
        for slot in range(first, first + count):
            if slot != MID:
                z_copies[slot].wait_recv()

    wait_group(0)
    forward(0)

    for i in (5, 6, 7):
        local[i].wait()
    for copy in c_copies:
        copy.wait_recv()
    low_half = (lane // 32) % 2 == 1
    for j in range(PAIRS // 2):
        total = None
        for g in range(2):
            q = 2 * j + g
            mat = coup[q]
            none = jnp.zeros((32, 32), BF16)
            stack = [mat, mat, none, none] if g == 0 else [none, none, mat, mat]
            basis = bx[fsrc_s[me * PAIRS + q] % 2]
            part = lax.dot_general(basis, jnp.concatenate(stack, axis=0), NT, preferred_element_type=F32)
            total = part if total is None else total + part
        high = total.astype(BF16).astype(F32)
        fg[j * 16 : (j + 1) * 16, :] = jnp.where(low_half, total - high, high).astype(BF16)

    wait_group(1)
    forward(1)
    wait_group(2)
    forward(2)

    def f_span(yo, co):
        return fg.at[pl.ds((yo * 2 + co) * 256, 256)]

    f_copies = {}
    for yo in (2, 1, 3):
        there = (NY - yo) % NY
        f_copies[there, 0] = send(f_span(0, 0), f_span(there, 0), fsem, there * 2, at(yo, 0, 0))
    f_copies[0, 1] = send(f_span(0, 0), f_span(0, 1), fsem, 1, at(0, 0, 1))
    for group in range(3):
        for yo in (1, 3, 2):
            y_copies[yo, 0, group].wait_recv()
            relay(yo, group)
    for group in range(3):
        for yo in (0, 1, 3, 2):
            y_copies[yo, 1, group].wait_recv()

    def p_span(g, yo, co):
        return pg.at[pl.ds((g * 8 + yo * 2 + co) * 128, 128)]

    local[8].wait()
    p_copies = {}
    for g in range(NCHUNK):
        for i in range(CHUNK):
            b = g * CHUNK + i
            s = nsrc_s[me * BLK + b]
            s_leaf = s // 2
            yo = (s_leaf // 32 + NY - y) % NY
            zo = ((s_leaf // 2) % 16 + NZ + MID - z) % NZ
            co = (s_leaf + c) % 2
            index = ((yo * 2 + co) * NZ + zo) * 2 + s % 2
            term = lax.dot_general(xg[index], blk[b], NT, preferred_element_type=F32)
            factor = jnp.exp2(jnp.full((16, 128), scale_s[b], jnp.int32).astype(F32))
            at_row = g * 1024 + i * 16
            pg[at_row : at_row + 16, :] = (term * factor).astype(BF16)
        for yo in (2, 1, 3):
            there = (NY - yo) % NY
            p_copies[g, there, 0] = send(
                p_span(g, 0, 0), p_span(g, there, 0), psem, g * 8 + there * 2, at(yo, 0, 0)
            )
        p_copies[g, 0, 1] = send(p_span(g, 0, 0), p_span(g, 0, 1), psem, g * 8 + 1, at(0, 0, 1))

    for yo in (1, 3, 2):
        f_copies[yo, 0].wait_recv()
        f_copies[yo, 1] = send(f_span(yo, 0), f_span(yo, 1), fsem, yo * 2 + 1, at(0, 0, 1))
    for yo in range(NY):
        f_copies[yo, 1].wait_recv()
    wide = lax.broadcasted_iota(jnp.int32, (2048, 128), 1)
    terms = fg[...]
    zero = jnp.zeros_like(terms)
    fa[...] = jnp.dot(kf[0], jnp.where(wide < 64, terms, zero), preferred_element_type=F32)
    fa[...] += jnp.dot(kf[1], jnp.where(wide < 64, zero, terms), preferred_element_type=F32)
    for zs in range(NZ):
        s = fa[zs * 32 : (zs + 1) * 32, :]
        s = s + pltpu.roll(s, 64, 1)
        s = s + pltpu.roll(s, 32, 1)
        v = jnp.where((lane // 32) % 2 == 0, s[0:16], s[16:32])
        high = v.astype(BF16).astype(F32)
        buf = zr_buf if zs == MID else zs_buf
        buf[zs, 32:48, :] = jnp.where(lane < 64, high, v - high).astype(BF16)

    for g in range(NCHUNK):
        for yo in (1, 3, 2):
            p_copies[g, yo, 0].wait_recv()
            p_copies[g, yo, 1] = send(
                p_span(g, yo, 0), p_span(g, yo, 1), psem, g * 8 + yo * 2 + 1, at(0, 0, 1)
            )
        if g > 0:
            for yo in range(NY):
                p_copies[g - 1, yo, 1].wait_recv()
            part = jnp.dot(
                kr[:, (g - 1) * 1024 : g * 1024], pg[(g - 1) * 1024 : g * 1024, :], preferred_element_type=F32
            )
            acc[...] = part if g == 1 else acc[...] + part
    for yo in range(NY):
        p_copies[NCHUNK - 1, yo, 1].wait_recv()
    last = (NCHUNK - 1) * 1024
    o_copies = []
    acc[...] += jnp.dot(kr[:, last:], pg[last:, :], preferred_element_type=F32)
    for zo in Z_ORDER:
        zs = (MID + zo) % NZ
        zs_buf[zs, 0:32, :] = acc[zs * 32 : (zs + 1) * 32, :].astype(BF16)
        there = (MID - zo) % NZ
        o_copies.append(send(zs_buf.at[zs], zr_buf.at[there], rsem, there, at(0, zo, 0)))
    total = acc[MID * 32 : (MID + 1) * 32, :]
    far = zr_buf[MID, 32:48, :].astype(F32)
    local[9].wait()
    for zo in reversed(range(15)):
        o_copies[zo].wait_recv()
        there = (MID - Z_ORDER[zo]) % NZ
        total = total + zr_buf[there, 0:32, :].astype(F32)
        far = far + zr_buf[there, 32:48, :].astype(F32)
    far = (far + pltpu.roll(far, 64, 1)).astype(BF16).astype(F32)
    both = jnp.concatenate(
        [jnp.where(lane < 32, far, 0.0), jnp.where((lane >= 32) & (lane < 64), far, 0.0)], axis=0
    ).astype(BF16)
    basis = jnp.concatenate([tb[0], tb[1], jnp.zeros((64, 128), BF16)], axis=0)
    total = total + jnp.dot(both, basis, preferred_element_type=F32)
    out[:, 0:128] = total[0:16]
    out[:, 128:256] = total[16:32]
    for copy in started:
        copy.wait_send()


def per_device(
    coeffs, near_blocks, near_scale, near_target, near_source, src_basis, tgt_basis, couplings, far_target, far_source
):
    dma = pltpu.SemaphoreType.DMA
    vmem, smem = pltpu.VMEM, pltpu.SMEM
    return pl.pallas_call(
        kernel,
        out_shape=jax.ShapeDtypeStruct((16, 256), F32),
        in_specs=[pl.BlockSpec(memory_space=pl.ANY)] * 10,
        out_specs=pl.BlockSpec(memory_space=pltpu.VMEM),
        scratch_shapes=[
            vmem((16, 256), BF16),
            vmem((BLK, 128, 128), BF16),
            smem((BLK,), jnp.int32),
            vmem((40, 128), jnp.int32),
            smem((5120,), jnp.int32),
            vmem((2, 32, 128), BF16),
            vmem((2, 32, 128), BF16),
            vmem((PAIRS, 32, 32), BF16),
            vmem((32, 128), jnp.int32),
            smem((4096,), jnp.int32),
            vmem((256, 16, 128), BF16),
            vmem((NCHUNK * 1024, 128), BF16),
            vmem((2048, 128), BF16),
            vmem((2, 16, 32), BF16),
            vmem((16, BLK * 16), F32),
            vmem((2, 16, 256), F32),
            vmem((512, 128), F32),
            vmem((512, NCHUNK * 1024), BF16),
            vmem((2, 512, 2048), BF16),
            vmem((512, 128), F32),
            vmem((512, 128), F32),
            vmem((NZ, 48, 128), BF16),
            vmem((NZ, 48, 128), BF16),
            dma((10,)),
            dma((2, NZ)),
            dma((2, 24)),
            dma((2, 3)),
            dma((2, 8)),
            dma((2, NCHUNK * 8)),
            dma((2, NZ)),
        ],
        compiler_params=pltpu.CompilerParams(
            collective_id=0, has_side_effects=True, vmem_limit_bytes=40 * 1024 * 1024
        ),
        cost_estimate=pl.CostEstimate(flops=10**9, bytes_accessed=2 * 10**6, transcendentals=0),
        name="near_far_operator",
    )(
        coeffs, near_blocks, near_scale, near_target.reshape(40, 128), near_source, src_basis, tgt_basis,
        couplings, far_target.reshape(32, 128), far_source,
    )


def solution(mesh):
    placed = (
        P("rhs", "leaf"),
        P("leaf", None, None),
        P("leaf"),
        P(),
        P(),
        P("leaf", None, None),
        P("leaf", None, None),
        P(("leaf", "rhs"), None, None),
        P(),
        P(),
    )
    return jax.shard_map(
        per_device, mesh=mesh, in_specs=placed, out_specs=P("rhs", "leaf"), check_vma=False
    )
```

```python
import jax
import jax.numpy as jnp
from jax import lax
from jax.experimental import pallas as pl
from jax.experimental.pallas import tpu as pltpu
from jax.sharding import PartitionSpec as P

MESH = pl.DeviceIdType.MESH
NY, NZ, NX = 4, 16, 4
MID = 8
NEAR = (0, 1, 15, 2, 14, 3, 13, 4, 12, 5, 11, 6, 10, 7, 9, 8)
BLK = 40
ROWS = BLK * 8
SPAN = 384
PAIRS = 32
SHARE = 8
SPLIT = 20
CLOSE = 7
Z_ORDER = (8, 7, 9, 6, 10, 5, 11, 4, 12, 3, 13, 2, 14, 1, 15)
PLACE = (0, 1, 3, 2)
RECV_NAMES = (
    "y_own", "z_close", "z_wide", "y_line1", "y_line2", "y_line3", "core", "coup", "far", "f_swap",
    "near0", "near1", "swap0", "swap1", "z_far", "z_near0", "z_near1",
)
RECV = {name: i for i, name in enumerate(RECV_NAMES)}
SEND = {name: max(0, i - 6) for i, name in enumerate(RECV_NAMES)}
F32, BF16 = jnp.float32, jnp.bfloat16
NT = (((1,), (1,)), ((), ()))


def kernel(
    coeffs, blocks, scale, ntgt, nsrc, src_basis, tgt_basis, couplings, ftgt, fsrc,
    out,
    x_in, blk, scale_s, ntgt_v, nsrc_s, sb, tb, cp_in, coup, ftgt_v, fsrc_s,
    xg, pg, fg, bx, t2n, t2f, v2, kr, kf, acc, acc_out, acc_in, fa, fown, f_out, f_in,
    zs_buf, zr_buf, fs_buf, fr_buf,
    lsem, rsem, ssem,
):
    me = lax.axis_index("leaf")
    x = lax.axis_index("rhs")
    y, z, c = me // 32, (me // 2) % 16, me % 2

    def leaf(yo, zo, co):
        return (((y + yo) % NY) * NZ + (z + zo) % NZ) * 2 + (c + co) % 2

    def at(yo, zo, co):
        return {"leaf": leaf(yo, zo, co)}

    x_copy = pltpu.make_async_copy(coeffs, x_in, lsem.at[9])
    x_copy.start()
    barrier = pltpu.get_barrier_semaphore()
    for zo in Z_ORDER:
        pl.semaphore_signal(barrier, inc=1, device_id=at(0, zo, 0), device_id_type=MESH)
    for yo in (2, 1, 3):
        pl.semaphore_signal(barrier, inc=1, device_id=at(yo, 0, 0), device_id_type=MESH)
    pl.semaphore_signal(barrier, inc=1, device_id=at(0, 0, 1), device_id_type=MESH)
    for xo in range(1, NX):
        pl.semaphore_signal(barrier, inc=1, device_id={"rhs": (x + xo) % NX}, device_id_type=MESH)

    local = []
    pairs = (
        (couplings, cp_in), (src_basis, sb), (ntgt, ntgt_v), (ftgt, ftgt_v), (fsrc, fsrc_s),
        (nsrc, nsrc_s), (scale, scale_s), (blocks, blk), (tgt_basis, tb),
    )
    for i, (a, b) in enumerate(pairs):
        copy = pltpu.make_async_copy(a, b, lsem.at[i])
        copy.start()
        local.append(copy)

    def copy_of(src, dst, name, device):
        return pltpu.make_async_remote_copy(
            src_ref=src, dst_ref=dst, send_sem=ssem.at[SEND[name]], recv_sem=rsem.at[RECV[name]],
            device_id=device, device_id_type=MESH,
        )

    def send(src, dst, name, device):
        copy_of(src, dst, name, device).start()

    def arrived(ref, name):
        copy_of(ref, ref, name, at(0, 0, 1)).wait_recv()

    def left(ref, name):
        copy_of(ref, ref, name, at(0, 0, 1)).wait_send()

    def x_tiles(first, count):
        return xg.at[pl.ds(first, count)]

    def close_at(slot, yo):
        return (slot * NY + yo) * 2

    def wide_at(slot, yo):
        return (CLOSE * NY + yo * (NZ - CLOSE) + slot - CLOSE) * 2

    wide = (NZ - CLOSE) * 2
    x_copy.wait()
    xg[0] = x_in[:, 0:128]
    xg[1] = x_in[:, 128:256]
    pl.semaphore_wait(barrier, 22)

    own = x_tiles(0, 2)
    for yo in (2, 1, 3):
        send(own, x_tiles(close_at(0, (NY - yo) % NY), 2), "y_own", at(yo, 0, 0))
    for zo in Z_ORDER:
        slot = NEAR.index((NZ - zo) % NZ)
        if slot < CLOSE:
            send(own, x_tiles(close_at(slot, 0), 2), "z_close", at(0, zo, 0))
        else:
            send(own, x_tiles(wide_at(slot, 0), 2), "z_wide", at(0, zo, 0))

    local[0].wait()
    i32 = lax.broadcasted_iota(jnp.int32, (32, 128), 0)
    lane32 = lax.broadcasted_iota(jnp.int32, (32, 128), 1)
    for t in range(SHARE // 4):
        packed = None
        for u in range(4):
            place = jnp.where(lane32 == i32 + u * 32, 1.0, 0.0).astype(BF16)
            part = jnp.dot(cp_in[t * 4 + u], place, preferred_element_type=F32)
            packed = part if packed is None else packed + part
        coup[x * (SHARE // 4) + t] = packed.astype(BF16)
    mine = coup.at[pl.ds(x * (SHARE // 4), SHARE // 4)]
    for xo in range(1, NX):
        send(mine, mine, "coup", {"rhs": (x + xo) % NX})

    local[1].wait()
    for k in range(2):
        four = jnp.concatenate([sb[k]] * 4, axis=0)
        part = lax.dot_general(xg[k], four, NT, preferred_element_type=F32)
        bx[k] = part.astype(BF16)

    local[2].wait()
    local[3].wait()
    lane = lax.broadcasted_iota(jnp.int32, (16, 128), 1)
    sub = lax.broadcasted_iota(jnp.int32, (16, 128), 0)
    near_rows = jnp.zeros((16, 128), jnp.int32)
    far_rows = jnp.zeros((16, 128), jnp.int32)
    for yo in range(NY):
        leaf_h = leaf(yo, 0, 0)
        first = leaf_h * BLK
        row, off = first // 128, first % 128
        after = jnp.minimum(row + 1, BLK - 1)
        one = jnp.broadcast_to(ntgt_v[pl.ds(row, 1), :], (16, 128))
        two = jnp.broadcast_to(ntgt_v[pl.ds(after, 1), :], (16, 128))
        both = pltpu.roll(jnp.where(lane >= off, one, two), (128 - off) % 128, 1)
        near_rows = jnp.where(sub == PLACE[yo], both, near_rows)
        frow, foff = leaf_h // 4, (leaf_h % 4) * 32
        fone = jnp.broadcast_to(ftgt_v[pl.ds(frow, 1), :], (16, 128))
        far_rows = jnp.where(sub == PLACE[yo], pltpu.roll(fone, (128 - foff) % 128, 1), far_rows)
    near_rows = near_rows.astype(F32).astype(BF16)
    far_rows = far_rows.astype(F32).astype(BF16)

    def spread(rows, width, step, start):
        b = lax.broadcasted_iota(jnp.int32, (128, width), 0)
        l = lax.broadcasted_iota(jnp.int32, (128, width), 1)
        pick = jnp.where(b == (l // 8) * step + start, 1.0, 0.0).astype(BF16)
        f = lax.broadcasted_iota(jnp.int32, (16, width), 1) % 8
        return jnp.dot(rows, pick, preferred_element_type=F32) * 8.0 + f.astype(F32)

    t2n[...] = spread(near_rows, SPAN, 1, 0)
    t2f[0] = spread(far_rows, 128, 2, 0)
    t2f[1] = spread(far_rows, 128, 2, 1)
    r = lax.broadcasted_iota(jnp.int32, (512, 128), 0)
    z_dst = (z + (r // 16) % 16 + (NZ - MID)) % NZ
    wanted = ((y * NZ + z_dst) * 2 + (c + r // 256) % 2) * 2 + (r // 8) % 2
    v2[...] = (wanted * 8 + r % 8).astype(F32)

    def build(i, carry):
        rows = pl.ds(pl.multiple_of(i * 32, 32), 32)
        want = v2[rows, :]
        for h in range(NY):
            for g in range(SPAN // 128):
                row = t2n[h : h + 1, g * 128 : (g + 1) * 128]
                to = h * SPAN + g * 128
                kr[rows, to : to + 128] = jnp.where(row == want, 1.0, 0.0).astype(BF16)
            for g in range(2):
                row = t2f[g, h : h + 1, :]
                kf[g, rows, h * 128 : (h + 1) * 128] = jnp.where(row == want, 1.0, 0.0).astype(BF16)
        return carry

    lax.fori_loop(0, 16, build, 0)
    for u in range(2):
        for h in range(NY):
            pg[u, h * SPAN + ROWS : (h + 1) * SPAN, :] = jnp.zeros((SPAN - ROWS, 128), BF16)

    arrived(x_tiles(2, 6), "y_own")
    for zo in (3, 13, 2, 14, 1, 15):
        slot = NEAR.index((NZ - zo) % NZ)
        send(x_tiles(2, 6), x_tiles(close_at(slot, 1), 6), "z_close", at(0, zo, 0))

    for i in (4, 5, 6):
        local[i].wait()
    arrived(coup.at[pl.ds(0, 6)], "coup")
    low_half = (lane // 32) % 2 == 1
    none = jnp.zeros((32, 128), BF16)
    for j in range(0, PAIRS // 2, 2):
        two = []
        for jj in (j, j + 1):
            total = None
            for g in range(2):
                q = 2 * jj + g
                mat = coup[q // 4]
                stack = [mat, mat, none, none] if g == 0 else [none, none, mat, mat]
                basis = bx[fsrc_s[me * PAIRS + q] % 2]
                basis = jnp.where(lane // 32 == q % 4, basis, jnp.zeros_like(basis))
                part = lax.dot_general(basis, jnp.concatenate(stack, axis=0), NT, preferred_element_type=F32)
                total = part if total is None else total + part
            high = total.astype(BF16).astype(F32)
            two.append(jnp.where(low_half, total - high, high))
        for u in range(2):
            half = jnp.concatenate([t[u * 8 : (u + 1) * 8] for t in two], axis=0)
            fg[j * 8 : (j + 2) * 8, u * 128 : (u + 1) * 128] = half.astype(BF16)

    for yo in (2, 1, 3):
        there = PLACE[(NY - yo) % NY]
        send(fg.at[pl.ds(0, 128)], fg.at[pl.ds(there * 128, 128)], "far", at(yo, 0, 0))

    line = x_tiles(wide_at(CLOSE, 0), wide)
    arrived(line, "z_wide")
    for yo in (2, 1, 3):
        there = (NY - yo) % NY
        send(line, x_tiles(wide_at(CLOSE, there), wide), "y_line%d" % there, at(yo, 0, 0))
    send(line, x_tiles(128 + wide_at(CLOSE, 0), wide), "core", at(0, 0, 1))
    arrived(x_tiles(8, 48), "z_close")
    send(x_tiles(0, 56), x_tiles(128, 56), "core", at(0, 0, 1))

    def halves(v):
        high = v.astype(BF16).astype(F32)
        return jnp.where(lax.broadcasted_iota(jnp.int32, v.shape, 1) < 64, high, v - high).astype(BF16)

    arrived(fg.at[pl.ds(0, 384)], "far")
    first_pair = lax.broadcasted_iota(jnp.int32, (512, 256), 1) % 128 < 64
    terms = fg[...]
    zero = jnp.zeros_like(terms)
    fa[...] = jnp.dot(kf[0], jnp.where(first_pair, terms, zero), preferred_element_type=F32)
    fa[...] += jnp.dot(kf[1], jnp.where(first_pair, zero, terms), preferred_element_type=F32)
    even = (lane[0:8] // 32) % 2 == 0
    for part in (1, 0):
        for zs in range(NZ):
            columns = []
            for u in range(2):
                s = fa[part * 256 + zs * 16 : part * 256 + (zs + 1) * 16, u * 128 : (u + 1) * 128]
                s = s + pltpu.roll(s, 64, 1)
                s = s + pltpu.roll(s, 32, 1)
                columns.append(jnp.where(even, s[0:8], s[8:16]))
            v = jnp.concatenate(columns, axis=0)
            if part == 1:
                f_out[zs * 16 : (zs + 1) * 16, :] = halves(v)
            else:
                fown[zs * 16 : (zs + 1) * 16, :] = v
        if part == 1:
            send(f_out, f_in, "f_swap", at(0, 0, 1))

    for yo in (1, 3, 2):
        line = wide_at(CLOSE, yo)
        arrived(x_tiles(line, wide), "y_line%d" % yo)
        send(x_tiles(line, wide), x_tiles(128 + line, wide), "core", at(0, 0, 1))
    arrived(x_tiles(128, 128), "core")

    def products(u, first, count):
        for yo in (2, 1, 3):
            there = PLACE[(NY - yo) % NY]
            rows = pl.ds(first * 8, count * 8)
            send(pg.at[u, rows], pg.at[u, pl.ds(there * SPAN + first * 8, count * 8)], "near%d" % u, at(yo, 0, 0))

    local[7].wait()
    for b in range(0, BLK, 2):
        two = []
        for bb in (b, b + 1):
            s = nsrc_s[me * BLK + bb]
            s_leaf = s // 2
            yo = (s_leaf // 32 + NY - y) % NY
            zo = ((s_leaf // 2) % 16 + NZ - z) % NZ
            zo = jnp.where(zo == 0, 0, jnp.where(zo <= 8, 2 * zo - 1, 2 * (NZ - zo)))
            co = (s_leaf + c) % 2
            tile = jnp.where(zo < CLOSE, zo * NY + yo, CLOSE * NY + yo * (NZ - CLOSE) + zo - CLOSE)
            index = co * 128 + tile * 2 + s % 2
            term = lax.dot_general(xg[index], blk[bb], NT, preferred_element_type=F32)
            two.append(term * jnp.exp2(jnp.full((16, 128), scale_s[bb], jnp.int32).astype(F32)))
        for u in range(2):
            half = jnp.concatenate([t[u * 8 : (u + 1) * 8] for t in two], axis=0)
            pg[u, b * 8 : (b + 2) * 8, :] = half.astype(BF16)
        if b + 2 == SPLIT:
            products(0, 0, SPLIT)
    products(0, SPLIT, BLK - SPLIT)
    products(1, 0, BLK)

    def to_all_z(src, dst, name):
        for zo in Z_ORDER:
            slot, there = (MID + zo) % NZ, (MID - zo) % NZ
            send(src.at[pl.ds(slot * 16, 16)], dst.at[pl.ds(there * 16, 16)], name, at(0, zo, 0))

    def from_all_z(dst, name):
        arrived(dst.at[pl.ds(0, 240)], name)
        total = dst[0:16, :].astype(F32)
        for slot in range(1, NZ):
            total = total + dst[slot * 16 : (slot + 1) * 16, :].astype(F32)
        return total

    arrived(f_in, "f_swap")
    theirs = f_in[...].astype(F32)
    far_all = halves(fown[...] + theirs + pltpu.roll(theirs, 64, 1))
    fs_buf[...] = far_all
    fr_buf[MID * 16 : (MID + 1) * 16, :] = far_all[MID * 16 : (MID + 1) * 16, :]
    to_all_z(fs_buf, fr_buf, "z_far")

    for u in range(2):
        arrived(pg.at[u, pl.ds(0, 3 * ROWS)], "near%d" % u)
        acc_out[u] = jnp.dot(kr[256:512, :], pg[u], preferred_element_type=F32)
        send(acc_out.at[u], acc_in.at[u], "swap%d" % u, at(0, 0, 1))
        acc[u] = jnp.dot(kr[0:256, :], pg[u], preferred_element_type=F32)
        arrived(acc_in.at[u], "swap%d" % u)
        near_all = (acc[u] + acc_in[u]).astype(BF16)
        zs_buf[u] = near_all
        zr_buf[u, MID * 16 : (MID + 1) * 16, :] = near_all[MID * 16 : (MID + 1) * 16, :]
        to_all_z(zs_buf.at[u], zr_buf.at[u], "z_near%d" % u)
    left(x_tiles(0, 254), "y_own")
    left(coup.at[pl.ds(0, 6)], "coup")
    left(fg.at[pl.ds(0, 384)], "far")
    left(f_out, "f_swap")
    left(fs_buf.at[pl.ds(0, 240)], "z_far")
    for u in range(2):
        left(pg.at[u, pl.ds(0, 3 * ROWS)], "near%d" % u)
        left(acc_out.at[u], "swap%d" % u)
    left(zs_buf.at[0, pl.ds(0, 240)], "z_near0")
    local[8].wait()
    far = from_all_z(fr_buf, "z_far")
    far = (far + pltpu.roll(far, 64, 1)).astype(BF16).astype(F32)
    both = jnp.concatenate(
        [jnp.where(lane < 32, far, 0.0), jnp.where((lane >= 32) & (lane < 64), far, 0.0)], axis=0
    ).astype(BF16)
    basis = jnp.concatenate([tb[0], tb[1], jnp.zeros((64, 128), BF16)], axis=0)
    far = jnp.dot(both, basis, preferred_element_type=F32)
    for u in range(2):
        near = from_all_z(zr_buf.at[u], "z_near%d" % u)
        for k in range(2):
            out[u * 8 : (u + 1) * 8, k * 128 : (k + 1) * 128] = (
                near[k * 8 : (k + 1) * 8] + far[k * 16 + u * 8 : k * 16 + (u + 1) * 8]
            )
    left(zs_buf.at[1, pl.ds(0, 240)], "z_near1")


def per_device(
    coeffs, near_blocks, near_scale, near_target, near_source, src_basis, tgt_basis, couplings, far_target, far_source
):
    dma = pltpu.SemaphoreType.DMA
    vmem, smem = pltpu.VMEM, pltpu.SMEM
    return pl.pallas_call(
        kernel,
        out_shape=jax.ShapeDtypeStruct((16, 256), F32),
        in_specs=[pl.BlockSpec(memory_space=pl.ANY)] * 10,
        out_specs=pl.BlockSpec(memory_space=pltpu.VMEM),
        scratch_shapes=[
            vmem((16, 256), BF16),
            vmem((BLK, 128, 128), BF16),
            smem((BLK,), jnp.int32),
            vmem((40, 128), jnp.int32),
            smem((5120,), jnp.int32),
            vmem((2, 32, 128), BF16),
            vmem((2, 32, 128), BF16),
            vmem((SHARE, 32, 32), BF16),
            vmem((PAIRS // 4, 32, 128), BF16),
            vmem((32, 128), jnp.int32),
            smem((4096,), jnp.int32),
            vmem((256, 16, 128), BF16),
            vmem((2, NY * SPAN, 128), BF16),
            vmem((NY * 128, 256), BF16),
            vmem((2, 16, 128), BF16),
            vmem((16, SPAN), F32),
            vmem((2, 16, 128), F32),
            vmem((512, 128), F32),
            vmem((512, NY * SPAN), BF16),
            vmem((2, 512, 512), BF16),
            vmem((2, 256, 128), F32),
            vmem((2, 256, 128), F32),
            vmem((2, 256, 128), F32),
            vmem((512, 256), F32),
            vmem((256, 128), F32),
            vmem((256, 128), BF16),
            vmem((256, 128), BF16),
            vmem((2, 256, 128), BF16),
            vmem((2, 256, 128), BF16),
            vmem((256, 128), BF16),
            vmem((256, 128), BF16),
            dma((10,)),
            dma((len(RECV),)),
            dma((len(RECV) - 6,)),
        ],
        compiler_params=pltpu.CompilerParams(
            collective_id=0, has_side_effects=True, vmem_limit_bytes=60 * 1024 * 1024
        ),
        cost_estimate=pl.CostEstimate(flops=10**9, bytes_accessed=2 * 10**6, transcendentals=0),
        name="near_far_operator",
    )(
        coeffs, near_blocks, near_scale, near_target.reshape(40, 128), near_source, src_basis, tgt_basis,
        couplings, far_target.reshape(32, 128), far_source,
    )


def solution(mesh):
    placed = (
        P("rhs", "leaf"),
        P("leaf", None, None),
        P("leaf"),
        P(),
        P(),
        P("leaf", None, None),
        P("leaf", None, None),
        P(("leaf", "rhs"), None, None),
        P(),
        P(),
    )
    return jax.shard_map(
        per_device, mesh=mesh, in_specs=placed, out_specs=P("rhs", "leaf"), check_vma=False
    )
```

```python
import jax
import jax.numpy as jnp
from jax import lax
from jax.experimental import pallas as pl
from jax.experimental.pallas import tpu as pltpu
from jax.sharding import PartitionSpec as P

MESH = pl.DeviceIdType.MESH
NY, NZ, NX = 4, 16, 4
MID = 8
NEAR = (0, 1, 15, 2, 14, 3, 13, 4, 12, 5, 11, 6, 10, 7, 9, 8)
BLK = 40
ROWS = BLK * 8
PAIRS = 32
SHARE = 8
SPLITS = (0, 16, 32, BLK)
CLOSE = 8
LINES = ((CLOSE, 13 - CLOSE), (13, 3))
Z_ORDER = (8, 7, 9, 6, 10, 5, 11, 4, 12, 3, 13, 2, 14, 1, 15)
TO_Z = Z_ORDER + (0,)
FAR_AFTER = 1
PARTS = 8
PLACE = (0, 1, 3, 2)
RECV_NAMES = (
    "y_own", "z_close", "z_line0", "z_line1", "y_line10", "y_line20", "y_line30", "y_line11", "y_line21", "y_line31", "core", "coup", "far", "f_swap", "pair",
    "dense0", "dense1", "dense2", "dense3", "dense4", "dense5", "dense6", "dense7",
    "z_far", "z_near0", "z_near1", "z_near2", "z_near3",
)
RECV = {name: i for i, name in enumerate(RECV_NAMES)}
SEND = dict(zip(RECV_NAMES, (0, 0, 0, 0, 0, 0, 0, 0, 0, 0, 0, 1, 2, 3, 4, 5, 5, 5, 5, 5, 5, 5, 5, 6, 7, 7, 7, 7)))
F32, BF16 = jnp.float32, jnp.bfloat16
NT = (((1,), (1,)), ((), ()))


def kernel(
    coeffs, blocks, scale, ntgt, nsrc, src_basis, tgt_basis, couplings, ftgt, fsrc,
    out,
    x_in, blk, scale_s, ntgt_v, nsrc_s, sb, tb, cp_in, coup, ftgt_v, fsrc_s,
    xg, pp, fg, bx, t2n, t2f, kr, kf, acc, ys_buf, yr_buf, fa, fown, f_out, f_in,
    zs_buf, zr_buf, fs_buf, fr_buf,
    index_s, lsem, rsem, ssem,
):
    me = lax.axis_index("leaf")
    x = lax.axis_index("rhs")
    y, z, c = me // 32, (me // 2) % 16, me % 2

    def leaf(yo, zo, co):
        return (((y + yo) % NY) * NZ + (z + zo) % NZ) * 2 + (c + co) % 2

    def at(yo, zo, co):
        return {"leaf": leaf(yo, zo, co)}

    x_copy = pltpu.make_async_copy(coeffs, x_in, lsem.at[9])
    x_copy.start()
    barrier = pltpu.get_barrier_semaphore()
    for zo in Z_ORDER:
        pl.semaphore_signal(barrier, inc=1, device_id=at(0, zo, 0), device_id_type=MESH)
    for yo in (2, 1, 3):
        pl.semaphore_signal(barrier, inc=1, device_id=at(yo, 0, 0), device_id_type=MESH)
    pl.semaphore_signal(barrier, inc=1, device_id=at(0, 0, 1), device_id_type=MESH)
    for xo in range(1, NX):
        pl.semaphore_signal(barrier, inc=1, device_id={"rhs": (x + xo) % NX}, device_id_type=MESH)

    local = []
    pairs = (
        (couplings, cp_in), (src_basis, sb), (ntgt, ntgt_v), (ftgt, ftgt_v), (fsrc, fsrc_s),
        (nsrc, nsrc_s), (scale, scale_s), (blocks, blk), (tgt_basis, tb),
    )
    for i, (a, b) in enumerate(pairs):
        copy = pltpu.make_async_copy(a, b, lsem.at[i])
        copy.start()
        local.append(copy)

    def copy_of(src, dst, name, device):
        return pltpu.make_async_remote_copy(
            src_ref=src, dst_ref=dst, send_sem=ssem.at[SEND[name]], recv_sem=rsem.at[RECV[name]],
            device_id=device, device_id_type=MESH,
        )

    def send(src, dst, name, device):
        copy_of(src, dst, name, device).start()

    def arrived(ref, name):
        copy_of(ref, ref, name, at(0, 0, 1)).wait_recv()

    def left(ref, name):
        copy_of(ref, ref, name, at(0, 0, 1)).wait_send()

    def x_tiles(first, count):
        return xg.at[pl.ds(first, count)]

    def close_at(slot, yo):
        return (slot * NY + yo) * 2

    def wide_at(slot, yo):
        return (CLOSE * NY + yo * (NZ - CLOSE) + slot - CLOSE) * 2

    def line_of(core, yo, group):
        first, count = LINES[group]
        return x_tiles(core * 128 + wide_at(first, yo), count * 2)

    x_copy.wait()
    xg[0] = x_in[:, 0:128]
    xg[1] = x_in[:, 128:256]
    pl.semaphore_wait(barrier, 22)

    own = x_tiles(0, 2)
    for yo in (2, 1, 3):
        send(own, x_tiles(close_at(0, (NY - yo) % NY), 2), "y_own", at(yo, 0, 0))
    for zo in Z_ORDER:
        slot = NEAR.index((NZ - zo) % NZ)
        if slot < CLOSE:
            send(own, x_tiles(close_at(slot, 0), 2), "z_close", at(0, zo, 0))
        else:
            send(own, x_tiles(wide_at(slot, 0), 2), "z_line%d" % (slot >= 13), at(0, zo, 0))

    local[0].wait()
    i32 = lax.broadcasted_iota(jnp.int32, (32, 128), 0)
    lane32 = lax.broadcasted_iota(jnp.int32, (32, 128), 1)
    for t in range(SHARE // 4):
        packed = None
        for u in range(4):
            place = jnp.where(lane32 == i32 + u * 32, 1.0, 0.0).astype(BF16)
            part = jnp.dot(cp_in[t * 4 + u], place, preferred_element_type=F32)
            packed = part if packed is None else packed + part
        coup[x * (SHARE // 4) + t] = packed.astype(BF16)
    mine = coup.at[pl.ds(x * (SHARE // 4), SHARE // 4)]
    for xo in range(1, NX):
        send(mine, mine, "coup", {"rhs": (x + xo) % NX})

    local[1].wait()
    for k in range(2):
        four = jnp.concatenate([sb[k]] * 4, axis=0)
        part = lax.dot_general(xg[k], four, NT, preferred_element_type=F32)
        bx[k] = part.astype(BF16)

    local[2].wait()
    local[3].wait()
    lane = lax.broadcasted_iota(jnp.int32, (16, 128), 1)
    sub = lax.broadcasted_iota(jnp.int32, (16, 128), 0)
    first = (me // 2) * 2 * BLK
    row, off = first // 128, first % 128
    after = jnp.minimum(row + 1, BLK - 1)
    one = jnp.broadcast_to(ntgt_v[pl.ds(row, 1), :], (16, 128))
    two = jnp.broadcast_to(ntgt_v[pl.ds(after, 1), :], (16, 128))
    near_rows = pltpu.roll(jnp.where(lane >= off, one, two), (128 - off) % 128, 1)
    far_rows = jnp.zeros((16, 128), jnp.int32)
    for yo in range(NY):
        leaf_h = leaf(yo, 0, 0)
        frow, foff = leaf_h // 4, (leaf_h % 4) * 32
        fone = jnp.broadcast_to(ftgt_v[pl.ds(frow, 1), :], (16, 128))
        far_rows = jnp.where(sub == PLACE[yo], pltpu.roll(fone, (128 - foff) % 128, 1), far_rows)
    near_rows = near_rows.astype(F32).astype(BF16)
    far_rows = far_rows.astype(F32).astype(BF16)

    def spread(rows, width, step, start):
        b = lax.broadcasted_iota(jnp.int32, (128, width), 0)
        l = lax.broadcasted_iota(jnp.int32, (128, width), 1)
        pick = jnp.where(b == (l // 8) * step + start, 1.0, 0.0).astype(BF16)
        f = lax.broadcasted_iota(jnp.int32, (16, width), 1) % 8
        return jnp.dot(rows, pick, preferred_element_type=F32) * 8.0 + f.astype(F32)

    t2n[...] = spread(near_rows, 2 * ROWS, 1, 0)
    t2f[0] = spread(far_rows, 128, 2, 0)
    t2f[1] = spread(far_rows, 128, 2, 1)
    in_16 = sub.astype(F32)

    def ones(row, leaf_to):
        return jnp.where(row == in_16 + leaf_to * 16.0, 1.0, 0.0).astype(BF16)

    far_lanes = [[jnp.broadcast_to(t2f[g, h : h + 1, :], (16, 128)) for h in range(NY)] for g in range(2)]

    def build_far(i, carry):
        for part in range(2):
            rows = pl.ds(pl.multiple_of(part * 256 + i * 16, 16), 16)
            leaf_to = ((y * NZ + (z + i + NZ - MID) % NZ) * 2 + (c + part) % 2).astype(F32)
            for g in range(2):
                for h in range(NY):
                    kf[g, rows, h * 128 : (h + 1) * 128] = ones(far_lanes[g][h], leaf_to)
        return carry

    near_lanes = [jnp.broadcast_to(t2n[0:1, g * 128 : (g + 1) * 128], (16, 128)) for g in range(2 * ROWS // 128)]

    def build_near(i, carry):
        p, yo = i // NY, i % NY
        for slot in range(2):
            zo = MID + p if slot == 0 else MID - 1 - p
            rows = pl.ds(pl.multiple_of(i * 32 + slot * 16, 16), 16)
            leaf_to = ((((y + yo) % NY) * NZ + (z + zo) % NZ) * 2 + c).astype(F32)
            for g, row in enumerate(near_lanes):
                kr[rows, g * 128 : (g + 1) * 128] = ones(row, leaf_to)
        return carry

    lax.fori_loop(0, 16, build_far, 0)
    lax.fori_loop(0, PARTS * NY, build_near, 0)

    arrived(x_tiles(2, 6), "y_own")
    for zo in Z_ORDER[16 - CLOSE :]:
        slot = NEAR.index((NZ - zo) % NZ)
        send(x_tiles(2, 6), x_tiles(close_at(slot, 1), 6), "z_close", at(0, zo, 0))

    for i in (4, 5, 6):
        local[i].wait()
    arrived(coup.at[pl.ds(0, 6)], "coup")
    low_half = (lane // 32) % 2 == 1
    none = jnp.zeros((32, 128), BF16)
    for j in range(0, PAIRS // 2, 2):
        two = []
        for jj in (j, j + 1):
            total = None
            for g in range(2):
                q = 2 * jj + g
                mat = coup[q // 4]
                stack = [mat, mat, none, none] if g == 0 else [none, none, mat, mat]
                basis = bx[fsrc_s[me * PAIRS + q] % 2]
                basis = jnp.where(lane // 32 == q % 4, basis, jnp.zeros_like(basis))
                part = lax.dot_general(basis, jnp.concatenate(stack, axis=0), NT, preferred_element_type=F32)
                total = part if total is None else total + part
            high = total.astype(BF16).astype(F32)
            two.append(jnp.where(low_half, total - high, high))
        for u in range(2):
            half = jnp.concatenate([t[u * 8 : (u + 1) * 8] for t in two], axis=0)
            fg[j * 8 : (j + 2) * 8, u * 128 : (u + 1) * 128] = half.astype(BF16)

    for yo in (2, 1, 3):
        there = PLACE[(NY - yo) % NY]
        send(fg.at[pl.ds(0, 128)], fg.at[pl.ds(there * 128, 128)], "far", at(yo, 0, 0))

    def find(bb, carry):
        s = nsrc_s[me * BLK + bb]
        s_leaf = s // 2
        yo = (s_leaf // 32 + NY - y) % NY
        zo = ((s_leaf // 2) % 16 + NZ - z) % NZ
        zo = jnp.where(zo == 0, 0, jnp.where(zo <= 8, 2 * zo - 1, 2 * (NZ - zo)))
        co = (s_leaf + c) % 2
        tile = jnp.where(zo < CLOSE, zo * NY + yo, CLOSE * NY + yo * (NZ - CLOSE) + zo - CLOSE)
        index_s[bb] = co * 128 + tile * 2 + s % 2
        return carry

    lax.fori_loop(0, BLK, find, 0)
    for group in range(2):
        line = line_of(0, 0, group)
        arrived(line, "z_line%d" % group)
        for yo in (2, 1, 3):
            there = (NY - yo) % NY
            send(line, line_of(0, there, group), "y_line%d%d" % (there, group), at(yo, 0, 0))
        send(line, line_of(1, 0, group), "core", at(0, 0, 1))
    arrived(x_tiles(8, (CLOSE - 1) * 8), "z_close")
    send(x_tiles(0, CLOSE * 8), x_tiles(128, CLOSE * 8), "core", at(0, 0, 1))

    def halves(v):
        high = v.astype(BF16).astype(F32)
        return jnp.where(lax.broadcasted_iota(jnp.int32, v.shape, 1) < 64, high, v - high).astype(BF16)

    arrived(fg.at[pl.ds(0, 384)], "far")
    first_pair = lax.broadcasted_iota(jnp.int32, (512, 256), 1) % 128 < 64
    terms = fg[...]
    zero = jnp.zeros_like(terms)
    fa[...] = jnp.dot(kf[0], jnp.where(first_pair, terms, zero), preferred_element_type=F32)
    fa[...] += jnp.dot(kf[1], jnp.where(first_pair, zero, terms), preferred_element_type=F32)
    even = (lane[0:8] // 32) % 2 == 0
    for part in (1, 0):
        for zs in range(NZ):
            columns = []
            for u in range(2):
                s = fa[part * 256 + zs * 16 : part * 256 + (zs + 1) * 16, u * 128 : (u + 1) * 128]
                s = s + pltpu.roll(s, 64, 1)
                s = s + pltpu.roll(s, 32, 1)
                columns.append(jnp.where(even, s[0:8], s[8:16]))
            v = jnp.concatenate(columns, axis=0)
            if part == 1:
                f_out[zs * 16 : (zs + 1) * 16, :] = halves(v)
            else:
                fown[zs * 16 : (zs + 1) * 16, :] = v
        if part == 1:
            send(f_out, f_in, "f_swap", at(0, 0, 1))

    for group in range(2):
        for yo in (1, 3, 2):
            line = line_of(0, yo, group)
            arrived(line, "y_line%d%d" % (yo, group))
            send(line, line_of(1, yo, group), "core", at(0, 0, 1))
    arrived(x_tiles(128, 128), "core")

    def share(first, count):
        rows = pl.ds(pl.multiple_of(c * ROWS + first * 8, 16), count * 8)
        send(pp.at[:, rows], pp.at[:, rows], "pair", at(0, 0, 1))

    local[7].wait()
    for b in range(0, BLK, 2):
        two = []
        for bb in (b, b + 1):
            index = index_s[bb]
            term = lax.dot_general(xg[index], blk[bb], NT, preferred_element_type=F32)
            two.append(term * jnp.exp2(jnp.full((16, 128), scale_s[bb], jnp.int32).astype(F32)))
        rows = pl.ds(pl.multiple_of(c * ROWS + b * 8, 16), 16)
        for u in range(2):
            half = jnp.concatenate([t[u * 8 : (u + 1) * 8] for t in two], axis=0)
            high = half.astype(BF16)
            pp[0, rows, u * 128 : (u + 1) * 128] = high
            pp[1, rows, u * 128 : (u + 1) * 128] = (half - high.astype(F32)).astype(BF16)
        if b + 2 in SPLITS:
            first = SPLITS[SPLITS.index(b + 2) - 1]
            share(first, b + 2 - first)

    arrived(pp.at[:, pl.ds(0, ROWS)], "pair")
    for p in range(PARTS):
        part = kr[p * 128 : (p + 1) * 128, :]
        sums = jnp.dot(part, pp[0], preferred_element_type=F32)
        sums = sums + jnp.dot(part, pp[1], preferred_element_type=F32)
        acc[p] = sums[0:32]
        for yo in range(1, NY):
            ys_buf[p, yo] = sums[yo * 32 : (yo + 1) * 32].astype(BF16)
        for yo in (2, 1, 3):
            send(ys_buf.at[p, yo], yr_buf.at[p, (NY - yo) % NY], "dense%d" % p, at(yo, 0, 0))
        if p == FAR_AFTER:
            arrived(f_in, "f_swap")
            theirs = f_in[...].astype(F32)
            far_all = halves(fown[...] + theirs + pltpu.roll(theirs, 64, 1))
            fs_buf[...] = far_all
            fr_buf[MID * 16 : (MID + 1) * 16, :] = far_all[MID * 16 : (MID + 1) * 16, :]
            for zo in Z_ORDER:
                slot, there = (MID + zo) % NZ, (MID - zo) % NZ
                send(fs_buf.at[pl.ds(slot * 16, 16)], fr_buf.at[pl.ds(there * 16, 16)], "z_far", at(0, zo, 0))


    for p in range(PARTS):
        arrived(yr_buf.at[p, pl.ds(1, 3)], "dense%d" % p)
        total = acc[p]
        for yo in range(1, NY):
            total = total + yr_buf[p, yo].astype(F32)
        total = total.astype(BF16)
        zs_buf[p * 32 : (p + 1) * 32, :] = total
        for i in range(2):
            zo = TO_Z[p * 2 + i]
            if zo == 0:
                zr_buf[(p * 2 + i) * 16 : (p * 2 + i + 1) * 16, :] = total[i * 16 : (i + 1) * 16]
            else:
                there = TO_Z.index(NZ - zo)
                send(
                    zs_buf.at[pl.ds((p * 2 + i) * 16, 16)], zr_buf.at[pl.ds(there * 16, 16)],
                    "z_near%d" % (there // 4), at(0, zo, 0),
                )
    left(x_tiles(0, 254), "y_own")
    left(coup.at[pl.ds(0, 6)], "coup")
    left(fg.at[pl.ds(0, 384)], "far")
    left(f_out, "f_swap")
    left(fs_buf.at[pl.ds(0, 240)], "z_far")
    left(pp.at[:, pl.ds(0, ROWS)], "pair")
    left(ys_buf.at[:, pl.ds(1, 3)], "dense0")
    local[8].wait()
    arrived(fr_buf.at[pl.ds(0, 240)], "z_far")
    far = fr_buf[0:16, :].astype(F32)
    for slot in range(1, NZ):
        far = far + fr_buf[slot * 16 : (slot + 1) * 16, :].astype(F32)
    far = (far + pltpu.roll(far, 64, 1)).astype(BF16).astype(F32)
    both = jnp.concatenate(
        [jnp.where(lane < 32, far, 0.0), jnp.where((lane >= 32) & (lane < 64), far, 0.0)], axis=0
    ).astype(BF16)
    basis = jnp.concatenate([tb[0], tb[1], jnp.zeros((64, 128), BF16)], axis=0)
    far = jnp.dot(both, basis, preferred_element_type=F32)
    near = zr_buf[240:256, :].astype(F32)
    for p in range(4):
        count = 4 if p < 3 else 3
        arrived(zr_buf.at[pl.ds(p * 64, count * 16)], "z_near%d" % p)
        for slot in range(p * 4, p * 4 + count):
            near = near + zr_buf[slot * 16 : (slot + 1) * 16, :].astype(F32)
    for u in range(2):
        for k in range(2):
            out[u * 8 : (u + 1) * 8, k * 128 : (k + 1) * 128] = (
                near[k * 8 : (k + 1) * 8, u * 128 : (u + 1) * 128]
                + far[k * 16 + u * 8 : k * 16 + (u + 1) * 8]
            )
    left(zs_buf.at[pl.ds(0, 240)], "z_near0")


def per_device(
    coeffs, near_blocks, near_scale, near_target, near_source, src_basis, tgt_basis, couplings, far_target, far_source
):
    dma = pltpu.SemaphoreType.DMA
    vmem, smem = pltpu.VMEM, pltpu.SMEM
    return pl.pallas_call(
        kernel,
        out_shape=jax.ShapeDtypeStruct((16, 256), F32),
        in_specs=[pl.BlockSpec(memory_space=pl.ANY)] * 10,
        out_specs=pl.BlockSpec(memory_space=pltpu.VMEM),
        scratch_shapes=[
            vmem((16, 256), BF16),
            vmem((BLK, 128, 128), BF16),
            smem((BLK,), jnp.int32),
            vmem((40, 128), jnp.int32),
            smem((5120,), jnp.int32),
            vmem((2, 32, 128), BF16),
            vmem((2, 32, 128), BF16),
            vmem((SHARE, 32, 32), BF16),
            vmem((PAIRS // 4, 32, 128), BF16),
            vmem((32, 128), jnp.int32),
            smem((4096,), jnp.int32),
            vmem((256, 16, 128), BF16),
            vmem((2, 2 * ROWS, 256), BF16),
            vmem((NY * 128, 256), BF16),
            vmem((2, 16, 128), BF16),
            vmem((16, 2 * ROWS), F32),
            vmem((2, 16, 128), F32),
            vmem((1024, 2 * ROWS), BF16),
            vmem((2, 512, 512), BF16),
            vmem((PARTS, 32, 256), F32),
            vmem((PARTS, NY, 32, 256), BF16),
            vmem((PARTS, NY, 32, 256), BF16),
            vmem((512, 256), F32),
            vmem((256, 128), F32),
            vmem((256, 128), BF16),
            vmem((256, 128), BF16),
            vmem((256, 256), BF16),
            vmem((256, 256), BF16),
            vmem((256, 128), BF16),
            vmem((256, 128), BF16),
            smem((BLK,), jnp.int32),
            dma((10,)),
            dma((len(RECV),)),
            dma((8,)),
        ],
        compiler_params=pltpu.CompilerParams(
            collective_id=0, has_side_effects=True, vmem_limit_bytes=60 * 1024 * 1024
        ),
        cost_estimate=pl.CostEstimate(flops=10**9, bytes_accessed=2 * 10**6, transcendentals=0),
        name="near_far_operator",
    )(
        coeffs, near_blocks, near_scale, near_target.reshape(40, 128), near_source, src_basis, tgt_basis,
        couplings, far_target.reshape(32, 128), far_source,
    )


def solution(mesh):
    placed = (
        P("rhs", "leaf"),
        P("leaf", None, None),
        P("leaf"),
        P(),
        P(),
        P("leaf", None, None),
        P("leaf", None, None),
        P(("leaf", "rhs"), None, None),
        P(),
        P(),
    )
    return jax.shard_map(
        per_device, mesh=mesh, in_specs=placed, out_specs=P("rhs", "leaf"), check_vma=False
    )
```

```python
import jax
import jax.numpy as jnp
from jax import lax
from jax.experimental import pallas as pl
from jax.experimental.pallas import tpu as pltpu
from jax.sharding import PartitionSpec as P

MESH = pl.DeviceIdType.MESH
NY, NZ, NX = 4, 16, 4
MID = 8
NEAR = (0, 1, 15, 2, 14, 3, 13, 4, 12, 5, 11, 6, 10, 7, 9, 8)
BLK = 40
ROWS = BLK * 8
PAIRS = 32
SHARE = 8
SPLITS = (0, 16, 32, BLK)
CLOSE = 7
LINES = ((CLOSE, 13 - CLOSE), (13, 3))
Z_ORDER = (8, 7, 9, 6, 10, 5, 11, 4, 12, 3, 13, 2, 14, 1, 15)
TO_Z = Z_ORDER + (0,)
FAR_AFTER = 1
DIRECT = (4, 12, 3, 13, 2, 14, 1, 15)
PARTS = 8
PLACE = (0, 1, 3, 2)
RECV_NAMES = (
    "y_own", "z_own", "z_close", "z_line0", "z_line1", "y_line10", "y_line20", "y_line30", "y_line11", "y_line21", "y_line31", "core", "coup", "far", "f_swap", "pair",
    "dense0", "dense1", "dense2", "dense3", "dense4", "dense5", "dense6", "dense7",
    "z_far", "z_near0", "z_near1", "z_near2", "z_near3",
)
RECV = {name: i for i, name in enumerate(RECV_NAMES)}
SEND = dict(zip(RECV_NAMES, (0, 0, 0, 0, 0, 0, 0, 0, 0, 0, 0, 0, 1, 2, 3, 4, 5, 5, 5, 5, 5, 5, 5, 5, 6, 7, 7, 7, 7)))
F32, BF16 = jnp.float32, jnp.bfloat16
NT = (((1,), (1,)), ((), ()))


def kernel(
    coeffs, blocks, scale, ntgt, nsrc, src_basis, tgt_basis, couplings, ftgt, fsrc,
    out,
    x_in, blk, scale_s, ntgt_v, nsrc_s, sb, tb, cp_in, coup, ftgt_v, fsrc_s,
    xg, pp, fg, bx, t2n, t2f, kr, kf, acc, ys_buf, yr_buf, fa, fown, f_out, f_in,
    zs_buf, zr_buf, fs_buf, fr_buf,
    index_s, lsem, rsem, ssem,
):
    me = lax.axis_index("leaf")
    x = lax.axis_index("rhs")
    y, z, c = me // 32, (me // 2) % 16, me % 2

    def leaf(yo, zo, co):
        return (((y + yo) % NY) * NZ + (z + zo) % NZ) * 2 + (c + co) % 2

    def at(yo, zo, co):
        return {"leaf": leaf(yo, zo, co)}

    x_copy = pltpu.make_async_copy(coeffs, x_in, lsem.at[9])
    x_copy.start()
    barrier = pltpu.get_barrier_semaphore()
    for zo in DIRECT:
        pl.semaphore_signal(barrier, inc=1, device_id=at(0, zo, 0), device_id_type=MESH)
    for yo in (2, 1, 3):
        pl.semaphore_signal(barrier, inc=1, device_id=at(yo, 0, 0), device_id_type=MESH)
    pl.semaphore_signal(barrier, inc=1, device_id=at(0, 0, 1), device_id_type=MESH)
    for xo in range(1, NX):
        pl.semaphore_signal(barrier, inc=1, device_id={"rhs": (x + xo) % NX}, device_id_type=MESH)

    local = []
    pairs = (
        (couplings, cp_in), (src_basis, sb), (ntgt, ntgt_v), (ftgt, ftgt_v), (fsrc, fsrc_s),
        (nsrc, nsrc_s), (scale, scale_s), (blocks, blk), (tgt_basis, tb),
    )
    for i, (a, b) in enumerate(pairs):
        copy = pltpu.make_async_copy(a, b, lsem.at[i])
        copy.start()
        local.append(copy)

    def copy_of(src, dst, name, device):
        return pltpu.make_async_remote_copy(
            src_ref=src, dst_ref=dst, send_sem=ssem.at[SEND[name]], recv_sem=rsem.at[RECV[name]],
            device_id=device, device_id_type=MESH,
        )

    def send(src, dst, name, device):
        copy_of(src, dst, name, device).start()

    def arrived(ref, name):
        copy_of(ref, ref, name, at(0, 0, 1)).wait_recv()

    def left(ref, name):
        copy_of(ref, ref, name, at(0, 0, 1)).wait_send()

    def x_tiles(first, count):
        return xg.at[pl.ds(first, count)]

    def close_at(slot, yo):
        return (slot * NY + yo) * 2

    def wide_at(slot, yo):
        return (CLOSE * NY + yo * (NZ - CLOSE) + slot - CLOSE) * 2

    def line_of(core, yo, group):
        first, count = LINES[group]
        return x_tiles(core * 128 + wide_at(first, yo), count * 2)

    x_copy.wait()
    xg[0] = x_in[:, 0:128]
    xg[1] = x_in[:, 128:256]
    pl.semaphore_wait(barrier, 15)

    own = x_tiles(0, 2)
    for yo in (2, 1, 3):
        send(own, x_tiles(close_at(0, (NY - yo) % NY), 2), "y_own", at(yo, 0, 0))
    def piece(zo):
        slot = NEAR.index(zo % NZ)
        return x_tiles(close_at(slot, 0) if slot < CLOSE else wide_at(slot, 0), 2)

    for zo in DIRECT:
        send(own, piece(-zo), "z_own", at(0, zo, 0))

    local[0].wait()
    i32 = lax.broadcasted_iota(jnp.int32, (32, 128), 0)
    lane32 = lax.broadcasted_iota(jnp.int32, (32, 128), 1)
    for t in range(SHARE // 4):
        packed = None
        for u in range(4):
            place = jnp.where(lane32 == i32 + u * 32, 1.0, 0.0).astype(BF16)
            part = jnp.dot(cp_in[t * 4 + u], place, preferred_element_type=F32)
            packed = part if packed is None else packed + part
        coup[x * (SHARE // 4) + t] = packed.astype(BF16)
    mine = coup.at[pl.ds(x * (SHARE // 4), SHARE // 4)]
    for xo in range(1, NX):
        send(mine, mine, "coup", {"rhs": (x + xo) % NX})

    local[1].wait()
    for k in range(2):
        four = jnp.concatenate([sb[k]] * 4, axis=0)
        part = lax.dot_general(xg[k], four, NT, preferred_element_type=F32)
        bx[k] = part.astype(BF16)

    local[2].wait()
    local[3].wait()
    lane = lax.broadcasted_iota(jnp.int32, (16, 128), 1)
    sub = lax.broadcasted_iota(jnp.int32, (16, 128), 0)
    first = (me // 2) * 2 * BLK
    row, off = first // 128, first % 128
    after = jnp.minimum(row + 1, BLK - 1)
    one = jnp.broadcast_to(ntgt_v[pl.ds(row, 1), :], (16, 128))
    two = jnp.broadcast_to(ntgt_v[pl.ds(after, 1), :], (16, 128))
    near_rows = pltpu.roll(jnp.where(lane >= off, one, two), (128 - off) % 128, 1)
    far_rows = jnp.zeros((16, 128), jnp.int32)
    for yo in range(NY):
        leaf_h = leaf(yo, 0, 0)
        frow, foff = leaf_h // 4, (leaf_h % 4) * 32
        fone = jnp.broadcast_to(ftgt_v[pl.ds(frow, 1), :], (16, 128))
        far_rows = jnp.where(sub == PLACE[yo], pltpu.roll(fone, (128 - foff) % 128, 1), far_rows)
    near_rows = near_rows.astype(F32).astype(BF16)
    far_rows = far_rows.astype(F32).astype(BF16)

    def spread(rows, width, step, start):
        b = lax.broadcasted_iota(jnp.int32, (128, width), 0)
        l = lax.broadcasted_iota(jnp.int32, (128, width), 1)
        pick = jnp.where(b == (l // 8) * step + start, 1.0, 0.0).astype(BF16)
        f = lax.broadcasted_iota(jnp.int32, (16, width), 1) % 8
        return jnp.dot(rows, pick, preferred_element_type=F32) * 8.0 + f.astype(F32)

    t2n[...] = spread(near_rows, 2 * ROWS, 1, 0)
    t2f[0] = spread(far_rows, 128, 2, 0)
    t2f[1] = spread(far_rows, 128, 2, 1)
    in_16 = sub.astype(F32)

    def ones(row, leaf_to):
        return jnp.where(row == in_16 + leaf_to * 16.0, 1.0, 0.0).astype(BF16)

    far_lanes = [[jnp.broadcast_to(t2f[g, h : h + 1, :], (16, 128)) for h in range(NY)] for g in range(2)]

    def build_far(i, carry):
        for part in range(2):
            rows = pl.ds(pl.multiple_of(part * 256 + i * 16, 16), 16)
            leaf_to = ((y * NZ + (z + i + NZ - MID) % NZ) * 2 + (c + part) % 2).astype(F32)
            for g in range(2):
                for h in range(NY):
                    kf[g, rows, h * 128 : (h + 1) * 128] = ones(far_lanes[g][h], leaf_to)
        return carry

    near_lanes = [jnp.broadcast_to(t2n[0:1, g * 128 : (g + 1) * 128], (16, 128)) for g in range(2 * ROWS // 128)]

    def build_near(i, carry):
        p, yo = i // NY, i % NY
        for slot in range(2):
            zo = MID + p if slot == 0 else MID - 1 - p
            rows = pl.ds(pl.multiple_of(i * 32 + slot * 16, 16), 16)
            leaf_to = ((((y + yo) % NY) * NZ + (z + zo) % NZ) * 2 + c).astype(F32)
            for g, row in enumerate(near_lanes):
                kr[rows, g * 128 : (g + 1) * 128] = ones(row, leaf_to)
        return carry

    lax.fori_loop(0, 16, build_far, 0)
    lax.fori_loop(0, PARTS * NY, build_near, 0)

    arrived(x_tiles(8, 16), "z_own")
    for zo in (4, 3, 13, 2, 14, 1, 15):
        far = zo + 4 if zo < MID else zo - 4
        send(piece(zo), piece(far), "z_line%d" % (NEAR.index(far) >= 13), at(0, zo - far, 0))
    def close_forward():
        arrived(x_tiles(2, 6), "y_own")
        for zo in Z_ORDER[16 - CLOSE :]:
            slot = NEAR.index((NZ - zo) % NZ)
            send(x_tiles(2, 6), x_tiles(close_at(slot, 1), 6), "z_close", at(0, zo, 0))

    pl.when(c == 0)(close_forward)
    for i in (4, 5, 6):
        local[i].wait()
    arrived(coup.at[pl.ds(0, 6)], "coup")
    low_half = (lane // 32) % 2 == 1
    none = jnp.zeros((32, 128), BF16)
    for j in range(0, PAIRS // 2, 2):
        two = []
        for jj in (j, j + 1):
            total = None
            for g in range(2):
                q = 2 * jj + g
                mat = coup[q // 4]
                stack = [mat, mat, none, none] if g == 0 else [none, none, mat, mat]
                basis = bx[fsrc_s[me * PAIRS + q] % 2]
                basis = jnp.where(lane // 32 == q % 4, basis, jnp.zeros_like(basis))
                part = lax.dot_general(basis, jnp.concatenate(stack, axis=0), NT, preferred_element_type=F32)
                total = part if total is None else total + part
            high = total.astype(BF16).astype(F32)
            two.append(jnp.where(low_half, total - high, high))
        for u in range(2):
            half = jnp.concatenate([t[u * 8 : (u + 1) * 8] for t in two], axis=0)
            fg[j * 8 : (j + 2) * 8, u * 128 : (u + 1) * 128] = half.astype(BF16)

    for yo in (2, 1, 3):
        there = PLACE[(NY - yo) % NY]
        send(fg.at[pl.ds(0, 128)], fg.at[pl.ds(there * 128, 128)], "far", at(yo, 0, 0))

    def find(bb, carry):
        s = nsrc_s[me * BLK + bb]
        s_leaf = s // 2
        yo = (s_leaf // 32 + NY - y) % NY
        zo = ((s_leaf // 2) % 16 + NZ - z) % NZ
        zo = jnp.where(zo == 0, 0, jnp.where(zo <= 8, 2 * zo - 1, 2 * (NZ - zo)))
        co = (s_leaf + c) % 2
        tile = jnp.where(zo < CLOSE, zo * NY + yo, CLOSE * NY + yo * (NZ - CLOSE) + zo - CLOSE)
        index_s[bb] = co * 128 + tile * 2 + s % 2
        return carry

    lax.fori_loop(0, BLK, find, 0)
    for group in range(2):
        line = line_of(0, 0, group)
        arrived(x_tiles(wide_at(13, 0), 6) if group else x_tiles(wide_at(9, 0), 8), "z_line%d" % group)
        for yo in (2, 1, 3):
            there = (NY - yo) % NY
            send(line, line_of(0, there, group), "y_line%d%d" % (there, group), at(yo, 0, 0))
        send(line, line_of(1, 0, group), "core", at(0, 0, 1))
    pl.when(c == 1)(close_forward)
    arrived(x_tiles(8, (CLOSE - 1) * 6), "z_close")
    send(x_tiles(0, CLOSE * 8), x_tiles(128, CLOSE * 8), "core", at(0, 0, 1))

    def halves(v):
        high = v.astype(BF16).astype(F32)
        return jnp.where(lax.broadcasted_iota(jnp.int32, v.shape, 1) < 64, high, v - high).astype(BF16)

    arrived(fg.at[pl.ds(0, 384)], "far")
    first_pair = lax.broadcasted_iota(jnp.int32, (512, 256), 1) % 128 < 64
    terms = fg[...]
    zero = jnp.zeros_like(terms)
    fa[...] = jnp.dot(kf[0], jnp.where(first_pair, terms, zero), preferred_element_type=F32)
    fa[...] += jnp.dot(kf[1], jnp.where(first_pair, zero, terms), preferred_element_type=F32)
    even = (lane[0:8] // 32) % 2 == 0
    for part in (1, 0):
        for zs in range(NZ):
            columns = []
            for u in range(2):
                s = fa[part * 256 + zs * 16 : part * 256 + (zs + 1) * 16, u * 128 : (u + 1) * 128]
                s = s + pltpu.roll(s, 64, 1)
                s = s + pltpu.roll(s, 32, 1)
                columns.append(jnp.where(even, s[0:8], s[8:16]))
            v = jnp.concatenate(columns, axis=0)
            if part == 1:
                f_out[zs * 16 : (zs + 1) * 16, :] = halves(v)
            else:
                fown[zs * 16 : (zs + 1) * 16, :] = v
        if part == 1:
            send(f_out, f_in, "f_swap", at(0, 0, 1))

    for group in range(2):
        for yo in (1, 3, 2):
            line = line_of(0, yo, group)
            arrived(line, "y_line%d%d" % (yo, group))
            send(line, line_of(1, yo, group), "core", at(0, 0, 1))
    arrived(x_tiles(128, 128), "core")

    def share(first, count):
        rows = pl.ds(pl.multiple_of(c * ROWS + first * 8, 16), count * 8)
        send(pp.at[:, rows], pp.at[:, rows], "pair", at(0, 0, 1))

    local[7].wait()
    for b in range(0, BLK, 2):
        two = []
        for bb in (b, b + 1):
            index = index_s[bb]
            term = lax.dot_general(xg[index], blk[bb], NT, preferred_element_type=F32)
            two.append(term * jnp.exp2(jnp.full((16, 128), scale_s[bb], jnp.int32).astype(F32)))
        rows = pl.ds(pl.multiple_of(c * ROWS + b * 8, 16), 16)
        for u in range(2):
            half = jnp.concatenate([t[u * 8 : (u + 1) * 8] for t in two], axis=0)
            high = half.astype(BF16)
            pp[0, rows, u * 128 : (u + 1) * 128] = high
            pp[1, rows, u * 128 : (u + 1) * 128] = (half - high.astype(F32)).astype(BF16)
        if b + 2 in SPLITS:
            first = SPLITS[SPLITS.index(b + 2) - 1]
            share(first, b + 2 - first)

    arrived(pp.at[:, pl.ds(0, ROWS)], "pair")
    for p in range(PARTS):
        part = kr[p * 128 : (p + 1) * 128, :]
        sums = jnp.dot(part, pp[0], preferred_element_type=F32)
        sums = sums + jnp.dot(part, pp[1], preferred_element_type=F32)
        acc[p] = sums[0:32]
        for yo in range(1, NY):
            ys_buf[p, yo] = sums[yo * 32 : (yo + 1) * 32].astype(BF16)
        for yo in (2, 1, 3):
            send(ys_buf.at[p, yo], yr_buf.at[p, (NY - yo) % NY], "dense%d" % p, at(yo, 0, 0))
        if p == FAR_AFTER:
            arrived(f_in, "f_swap")
            theirs = f_in[...].astype(F32)
            far_all = halves(fown[...] + theirs + pltpu.roll(theirs, 64, 1))
            fs_buf[...] = far_all
            fr_buf[MID * 16 : (MID + 1) * 16, :] = far_all[MID * 16 : (MID + 1) * 16, :]
            for zo in Z_ORDER:
                slot, there = (MID + zo) % NZ, (MID - zo) % NZ
                send(fs_buf.at[pl.ds(slot * 16, 16)], fr_buf.at[pl.ds(there * 16, 16)], "z_far", at(0, zo, 0))


    for p in range(PARTS):
        arrived(yr_buf.at[p, pl.ds(1, 3)], "dense%d" % p)
        total = acc[p]
        for yo in range(1, NY):
            total = total + yr_buf[p, yo].astype(F32)
        total = total.astype(BF16)
        zs_buf[p * 32 : (p + 1) * 32, :] = total
        for i in range(2):
            zo = TO_Z[p * 2 + i]
            if zo == 0:
                zr_buf[(p * 2 + i) * 16 : (p * 2 + i + 1) * 16, :] = total[i * 16 : (i + 1) * 16]
            else:
                there = TO_Z.index(NZ - zo)
                send(
                    zs_buf.at[pl.ds((p * 2 + i) * 16, 16)], zr_buf.at[pl.ds(there * 16, 16)],
                    "z_near%d" % (there // 4), at(0, zo, 0),
                )
    left(x_tiles(0, 254), "y_own")
    left(coup.at[pl.ds(0, 6)], "coup")
    left(fg.at[pl.ds(0, 384)], "far")
    left(f_out, "f_swap")
    left(fs_buf.at[pl.ds(0, 240)], "z_far")
    left(pp.at[:, pl.ds(0, ROWS)], "pair")
    left(ys_buf.at[:, pl.ds(1, 3)], "dense0")
    local[8].wait()
    arrived(fr_buf.at[pl.ds(0, 240)], "z_far")
    far = fr_buf[0:16, :].astype(F32)
    for slot in range(1, NZ):
        far = far + fr_buf[slot * 16 : (slot + 1) * 16, :].astype(F32)
    far = (far + pltpu.roll(far, 64, 1)).astype(BF16).astype(F32)
    both = jnp.concatenate(
        [jnp.where(lane < 32, far, 0.0), jnp.where((lane >= 32) & (lane < 64), far, 0.0)], axis=0
    ).astype(BF16)
    basis = jnp.concatenate([tb[0], tb[1], jnp.zeros((64, 128), BF16)], axis=0)
    far = jnp.dot(both, basis, preferred_element_type=F32)
    near = zr_buf[240:256, :].astype(F32)
    for p in range(4):
        count = 4 if p < 3 else 3
        arrived(zr_buf.at[pl.ds(p * 64, count * 16)], "z_near%d" % p)
        for slot in range(p * 4, p * 4 + count):
            near = near + zr_buf[slot * 16 : (slot + 1) * 16, :].astype(F32)
    for u in range(2):
        for k in range(2):
            out[u * 8 : (u + 1) * 8, k * 128 : (k + 1) * 128] = (
                near[k * 8 : (k + 1) * 8, u * 128 : (u + 1) * 128]
                + far[k * 16 + u * 8 : k * 16 + (u + 1) * 8]
            )
    left(zs_buf.at[pl.ds(0, 240)], "z_near0")


def per_device(
    coeffs, near_blocks, near_scale, near_target, near_source, src_basis, tgt_basis, couplings, far_target, far_source
):
    dma = pltpu.SemaphoreType.DMA
    vmem, smem = pltpu.VMEM, pltpu.SMEM
    return pl.pallas_call(
        kernel,
        out_shape=jax.ShapeDtypeStruct((16, 256), F32),
        in_specs=[pl.BlockSpec(memory_space=pl.ANY)] * 10,
        out_specs=pl.BlockSpec(memory_space=pltpu.VMEM),
        scratch_shapes=[
            vmem((16, 256), BF16),
            vmem((BLK, 128, 128), BF16),
            smem((BLK,), jnp.int32),
            vmem((40, 128), jnp.int32),
            smem((5120,), jnp.int32),
            vmem((2, 32, 128), BF16),
            vmem((2, 32, 128), BF16),
            vmem((SHARE, 32, 32), BF16),
            vmem((PAIRS // 4, 32, 128), BF16),
            vmem((32, 128), jnp.int32),
            smem((4096,), jnp.int32),
            vmem((256, 16, 128), BF16),
            vmem((2, 2 * ROWS, 256), BF16),
            vmem((NY * 128, 256), BF16),
            vmem((2, 16, 128), BF16),
            vmem((16, 2 * ROWS), F32),
            vmem((2, 16, 128), F32),
            vmem((1024, 2 * ROWS), BF16),
            vmem((2, 512, 512), BF16),
            vmem((PARTS, 32, 256), F32),
            vmem((PARTS, NY, 32, 256), BF16),
            vmem((PARTS, NY, 32, 256), BF16),
            vmem((512, 256), F32),
            vmem((256, 128), F32),
            vmem((256, 128), BF16),
            vmem((256, 128), BF16),
            vmem((256, 256), BF16),
            vmem((256, 256), BF16),
            vmem((256, 128), BF16),
            vmem((256, 128), BF16),
            smem((BLK,), jnp.int32),
            dma((10,)),
            dma((len(RECV),)),
            dma((8,)),
        ],
        compiler_params=pltpu.CompilerParams(
            collective_id=0, has_side_effects=True, vmem_limit_bytes=60 * 1024 * 1024
        ),
        cost_estimate=pl.CostEstimate(flops=10**9, bytes_accessed=2 * 10**6, transcendentals=0),
        name="near_far_operator",
    )(
        coeffs, near_blocks, near_scale, near_target.reshape(40, 128), near_source, src_basis, tgt_basis,
        couplings, far_target.reshape(32, 128), far_source,
    )


def solution(mesh):
    placed = (
        P("rhs", "leaf"),
        P("leaf", None, None),
        P("leaf"),
        P(),
        P(),
        P("leaf", None, None),
        P("leaf", None, None),
        P(("leaf", "rhs"), None, None),
        P(),
        P(),
    )
    return jax.shard_map(
        per_device, mesh=mesh, in_specs=placed, out_specs=P("rhs", "leaf"), check_vma=False
    )
```

```python
import jax
import jax.numpy as jnp
from jax import lax
from jax.experimental import pallas as pl
from jax.experimental.pallas import tpu as pltpu
from jax.sharding import PartitionSpec as P

MESH = pl.DeviceIdType.MESH
NY, NZ, NX = 4, 16, 4
MID = 8
NEAR = (0, 1, 15, 2, 14, 3, 13, 4, 12, 5, 11, 6, 10, 7, 9, 8)
BLK = 40
ROWS = BLK * 8
PAIRS = 32
SHARE = 8
SPLITS = (0, 16, 32, BLK)
CLOSE = 3
LINES = ((CLOSE, 9 - CLOSE), (9, 7))
Z_ORDER = (8, 7, 9, 6, 10, 5, 11, 4, 12, 3, 13, 2, 14, 1, 15)
TO_Z = Z_ORDER + (0,)
FAR_AFTER = 1
DIRECT = (4, 12, 3, 13, 2, 14, 1, 15)
PARTS = 8
PLACE = (0, 1, 3, 2)
RECV_NAMES = (
    "y_own", "z_own", "z_close", "z_line", "y_line10", "y_line20", "y_line30", "y_line11", "y_line21", "y_line31", "core", "coup", "far", "f_swap", "pair",
    "dense0", "dense1", "dense2", "dense3", "dense4", "dense5", "dense6", "dense7",
    "z_far", "z_near0", "z_near1", "z_near2", "z_near3",
)
RECV = {name: i for i, name in enumerate(RECV_NAMES)}
SEND = dict(zip(RECV_NAMES, (0, 0, 0, 0, 0, 0, 0, 0, 0, 0, 0, 1, 2, 3, 4, 5, 5, 5, 5, 5, 5, 5, 5, 6, 7, 7, 7, 7)))
F32, BF16 = jnp.float32, jnp.bfloat16
NT = (((1,), (1,)), ((), ()))


def kernel(
    coeffs, blocks, scale, ntgt, nsrc, src_basis, tgt_basis, couplings, ftgt, fsrc,
    out,
    x_in, blk, scale_s, ntgt_v, nsrc_s, sb, tb, cp_in, coup, ftgt_v, fsrc_s,
    xg, pp, fg, bx, t2n, t2f, kr, kf, acc, ys_buf, yr_buf, fa, fown, f_out, f_in,
    zs_buf, zr_buf, fs_buf, fr_buf,
    index_s, lsem, rsem, ssem,
):
    me = lax.axis_index("leaf")
    x = lax.axis_index("rhs")
    y, z, c = me // 32, (me // 2) % 16, me % 2

    def leaf(yo, zo, co):
        return (((y + yo) % NY) * NZ + (z + zo) % NZ) * 2 + (c + co) % 2

    def at(yo, zo, co):
        return {"leaf": leaf(yo, zo, co)}

    x_copy = pltpu.make_async_copy(coeffs, x_in, lsem.at[9])
    x_copy.start()
    barrier = pltpu.get_barrier_semaphore()
    for zo in DIRECT:
        pl.semaphore_signal(barrier, inc=1, device_id=at(0, zo, 0), device_id_type=MESH)
    for yo in (2, 1, 3):
        pl.semaphore_signal(barrier, inc=1, device_id=at(yo, 0, 0), device_id_type=MESH)
    pl.semaphore_signal(barrier, inc=1, device_id=at(0, 0, 1), device_id_type=MESH)
    for xo in range(1, NX):
        pl.semaphore_signal(barrier, inc=1, device_id={"rhs": (x + xo) % NX}, device_id_type=MESH)

    local = []
    pairs = (
        (couplings, cp_in), (src_basis, sb), (ntgt, ntgt_v), (ftgt, ftgt_v), (fsrc, fsrc_s),
        (nsrc, nsrc_s), (scale, scale_s), (blocks, blk), (tgt_basis, tb),
    )
    for i, (a, b) in enumerate(pairs):
        copy = pltpu.make_async_copy(a, b, lsem.at[i])
        copy.start()
        local.append(copy)

    def copy_of(src, dst, name, device):
        return pltpu.make_async_remote_copy(
            src_ref=src, dst_ref=dst, send_sem=ssem.at[SEND[name]], recv_sem=rsem.at[RECV[name]],
            device_id=device, device_id_type=MESH,
        )

    def send(src, dst, name, device):
        copy_of(src, dst, name, device).start()

    def arrived(ref, name):
        copy_of(ref, ref, name, at(0, 0, 1)).wait_recv()

    def left(ref, name):
        copy_of(ref, ref, name, at(0, 0, 1)).wait_send()

    def x_tiles(first, count):
        return xg.at[pl.ds(first, count)]

    def close_at(slot, yo):
        return (slot * NY + yo) * 2

    def wide_at(slot, yo):
        return (CLOSE * NY + yo * (NZ - CLOSE) + slot - CLOSE) * 2

    def line_of(core, yo, group):
        first, count = LINES[group]
        return x_tiles(core * 128 + wide_at(first, yo), count * 2)

    x_copy.wait()
    xg[0] = x_in[:, 0:128]
    xg[1] = x_in[:, 128:256]
    pl.semaphore_wait(barrier, 15)

    own = x_tiles(0, 2)
    for yo in (2, 1, 3):
        send(own, x_tiles(close_at(0, (NY - yo) % NY), 2), "y_own", at(yo, 0, 0))
    def piece(zo):
        slot = NEAR.index(zo % NZ)
        return x_tiles(close_at(slot, 0) if slot < CLOSE else wide_at(slot, 0), 2)

    for zo in DIRECT:
        send(own, piece(-zo), "z_own", at(0, zo, 0))

    local[0].wait()
    i32 = lax.broadcasted_iota(jnp.int32, (32, 128), 0)
    lane32 = lax.broadcasted_iota(jnp.int32, (32, 128), 1)
    for t in range(SHARE // 4):
        packed = None
        for u in range(4):
            place = jnp.where(lane32 == i32 + u * 32, 1.0, 0.0).astype(BF16)
            part = jnp.dot(cp_in[t * 4 + u], place, preferred_element_type=F32)
            packed = part if packed is None else packed + part
        coup[x * (SHARE // 4) + t] = packed.astype(BF16)
    mine = coup.at[pl.ds(x * (SHARE // 4), SHARE // 4)]
    for xo in range(1, NX):
        send(mine, mine, "coup", {"rhs": (x + xo) % NX})

    local[1].wait()
    for k in range(2):
        four = jnp.concatenate([sb[k]] * 4, axis=0)
        part = lax.dot_general(xg[k], four, NT, preferred_element_type=F32)
        bx[k] = part.astype(BF16)

    local[2].wait()
    local[3].wait()
    lane = lax.broadcasted_iota(jnp.int32, (16, 128), 1)
    sub = lax.broadcasted_iota(jnp.int32, (16, 128), 0)
    first = (me // 2) * 2 * BLK
    row, off = first // 128, first % 128
    after = jnp.minimum(row + 1, BLK - 1)
    one = jnp.broadcast_to(ntgt_v[pl.ds(row, 1), :], (16, 128))
    two = jnp.broadcast_to(ntgt_v[pl.ds(after, 1), :], (16, 128))
    near_rows = pltpu.roll(jnp.where(lane >= off, one, two), (128 - off) % 128, 1)
    far_rows = jnp.zeros((16, 128), jnp.int32)
    for yo in range(NY):
        leaf_h = leaf(yo, 0, 0)
        frow, foff = leaf_h // 4, (leaf_h % 4) * 32
        fone = jnp.broadcast_to(ftgt_v[pl.ds(frow, 1), :], (16, 128))
        far_rows = jnp.where(sub == PLACE[yo], pltpu.roll(fone, (128 - foff) % 128, 1), far_rows)
    near_rows = near_rows.astype(F32).astype(BF16)
    far_rows = far_rows.astype(F32).astype(BF16)

    def spread(rows, width, step, start):
        b = lax.broadcasted_iota(jnp.int32, (128, width), 0)
        l = lax.broadcasted_iota(jnp.int32, (128, width), 1)
        pick = jnp.where(b == (l // 8) * step + start, 1.0, 0.0).astype(BF16)
        f = lax.broadcasted_iota(jnp.int32, (16, width), 1) % 8
        return jnp.dot(rows, pick, preferred_element_type=F32) * 8.0 + f.astype(F32)

    t2n[...] = spread(near_rows, 2 * ROWS, 1, 0)
    t2f[0] = spread(far_rows, 128, 2, 0)
    t2f[1] = spread(far_rows, 128, 2, 1)
    in_16 = sub.astype(F32)

    def ones(row, leaf_to):
        return jnp.where(row == in_16 + leaf_to * 16.0, 1.0, 0.0).astype(BF16)

    far_lanes = [[jnp.broadcast_to(t2f[g, h : h + 1, :], (16, 128)) for h in range(NY)] for g in range(2)]

    def build_far(i, carry):
        for part in range(2):
            rows = pl.ds(pl.multiple_of(part * 256 + i * 16, 16), 16)
            leaf_to = ((y * NZ + (z + i + NZ - MID) % NZ) * 2 + (c + part) % 2).astype(F32)
            for g in range(2):
                for h in range(NY):
                    kf[g, rows, h * 128 : (h + 1) * 128] = ones(far_lanes[g][h], leaf_to)
        return carry

    near_lanes = [jnp.broadcast_to(t2n[0:1, g * 128 : (g + 1) * 128], (16, 128)) for g in range(2 * ROWS // 128)]

    def build_near(i, carry):
        p, yo = i // NY, i % NY
        for slot in range(2):
            zo = MID + p if slot == 0 else MID - 1 - p
            rows = pl.ds(pl.multiple_of(i * 32 + slot * 16, 16), 16)
            leaf_to = ((((y + yo) % NY) * NZ + (z + zo) % NZ) * 2 + c).astype(F32)
            for g, row in enumerate(near_lanes):
                kr[rows, g * 128 : (g + 1) * 128] = ones(row, leaf_to)
        return carry

    lax.fori_loop(0, 16, build_far, 0)
    lax.fori_loop(0, PARTS * NY, build_near, 0)

    arrived(x_tiles(8, 16), "z_own")
    for zo in (4, 3, 13, 2, 14, 1, 15):
        far = zo + 4 if zo < MID else zo - 4
        send(piece(zo), piece(far), "z_line", at(0, zo - far, 0))
    def line_out(group):
        line = line_of(0, 0, group)
        for yo in (2, 1, 3):
            there = (NY - yo) % NY
            send(line, line_of(0, there, group), "y_line%d%d" % (there, group), at(yo, 0, 0))
        send(line, line_of(1, 0, group), "core", at(0, 0, 1))

    line_out(0)

    def close_forward():
        arrived(x_tiles(2, 6), "y_own")
        for zo in Z_ORDER[16 - CLOSE :]:
            slot = NEAR.index((NZ - zo) % NZ)
            send(x_tiles(2, 6), x_tiles(close_at(slot, 1), 6), "z_close", at(0, zo, 0))

    pl.when(c == 0)(close_forward)
    for i in (4, 5, 6):
        local[i].wait()
    arrived(coup.at[pl.ds(0, 6)], "coup")
    low_half = (lane // 32) % 2 == 1
    none = jnp.zeros((32, 128), BF16)
    for j in range(0, PAIRS // 2, 2):
        two = []
        for jj in (j, j + 1):
            total = None
            for g in range(2):
                q = 2 * jj + g
                mat = coup[q // 4]
                stack = [mat, mat, none, none] if g == 0 else [none, none, mat, mat]
                basis = bx[fsrc_s[me * PAIRS + q] % 2]
                basis = jnp.where(lane // 32 == q % 4, basis, jnp.zeros_like(basis))
                part = lax.dot_general(basis, jnp.concatenate(stack, axis=0), NT, preferred_element_type=F32)
                total = part if total is None else total + part
            high = total.astype(BF16).astype(F32)
            two.append(jnp.where(low_half, total - high, high))
        for u in range(2):
            half = jnp.concatenate([t[u * 8 : (u + 1) * 8] for t in two], axis=0)
            fg[j * 8 : (j + 2) * 8, u * 128 : (u + 1) * 128] = half.astype(BF16)

    for yo in (2, 1, 3):
        there = PLACE[(NY - yo) % NY]
        send(fg.at[pl.ds(0, 128)], fg.at[pl.ds(there * 128, 128)], "far", at(yo, 0, 0))

    def find(bb, carry):
        s = nsrc_s[me * BLK + bb]
        s_leaf = s // 2
        yo = (s_leaf // 32 + NY - y) % NY
        zo = ((s_leaf // 2) % 16 + NZ - z) % NZ
        zo = jnp.where(zo == 0, 0, jnp.where(zo <= 8, 2 * zo - 1, 2 * (NZ - zo)))
        co = (s_leaf + c) % 2
        tile = jnp.where(zo < CLOSE, zo * NY + yo, CLOSE * NY + yo * (NZ - CLOSE) + zo - CLOSE)
        index_s[bb] = co * 128 + tile * 2 + s % 2
        return carry

    lax.fori_loop(0, BLK, find, 0)
    arrived(x_tiles(wide_at(9, 0), 14), "z_line")
    line_out(1)
    pl.when(c == 1)(close_forward)
    arrived(x_tiles(8, (CLOSE - 1) * 6), "z_close")
    send(x_tiles(0, CLOSE * 8), x_tiles(128, CLOSE * 8), "core", at(0, 0, 1))

    def halves(v):
        high = v.astype(BF16).astype(F32)
        return jnp.where(lax.broadcasted_iota(jnp.int32, v.shape, 1) < 64, high, v - high).astype(BF16)

    arrived(fg.at[pl.ds(0, 384)], "far")
    first_pair = lax.broadcasted_iota(jnp.int32, (512, 256), 1) % 128 < 64
    terms = fg[...]
    zero = jnp.zeros_like(terms)
    fa[...] = jnp.dot(kf[0], jnp.where(first_pair, terms, zero), preferred_element_type=F32)
    fa[...] += jnp.dot(kf[1], jnp.where(first_pair, zero, terms), preferred_element_type=F32)
    even = (lane[0:8] // 32) % 2 == 0
    for part in (1, 0):
        for zs in range(NZ):
            columns = []
            for u in range(2):
                s = fa[part * 256 + zs * 16 : part * 256 + (zs + 1) * 16, u * 128 : (u + 1) * 128]
                s = s + pltpu.roll(s, 64, 1)
                s = s + pltpu.roll(s, 32, 1)
                columns.append(jnp.where(even, s[0:8], s[8:16]))
            v = jnp.concatenate(columns, axis=0)
            if part == 1:
                f_out[zs * 16 : (zs + 1) * 16, :] = halves(v)
            else:
                fown[zs * 16 : (zs + 1) * 16, :] = v
        if part == 1:
            send(f_out, f_in, "f_swap", at(0, 0, 1))

    for group in range(2):
        for yo in (1, 3, 2):
            line = line_of(0, yo, group)
            arrived(line, "y_line%d%d" % (yo, group))
            send(line, line_of(1, yo, group), "core", at(0, 0, 1))
    arrived(x_tiles(128, 128), "core")

    def share(first, count):
        rows = pl.ds(pl.multiple_of(c * ROWS + first * 8, 16), count * 8)
        send(pp.at[:, rows], pp.at[:, rows], "pair", at(0, 0, 1))

    local[7].wait()
    for b in range(0, BLK, 2):
        two = []
        for bb in (b, b + 1):
            index = index_s[bb]
            term = lax.dot_general(xg[index], blk[bb], NT, preferred_element_type=F32)
            two.append(term * jnp.exp2(jnp.full((16, 128), scale_s[bb], jnp.int32).astype(F32)))
        rows = pl.ds(pl.multiple_of(c * ROWS + b * 8, 16), 16)
        for u in range(2):
            half = jnp.concatenate([t[u * 8 : (u + 1) * 8] for t in two], axis=0)
            high = half.astype(BF16)
            pp[0, rows, u * 128 : (u + 1) * 128] = high
            pp[1, rows, u * 128 : (u + 1) * 128] = (half - high.astype(F32)).astype(BF16)
        if b + 2 in SPLITS:
            first = SPLITS[SPLITS.index(b + 2) - 1]
            share(first, b + 2 - first)

    arrived(pp.at[:, pl.ds(0, ROWS)], "pair")
    for p in range(PARTS):
        part = kr[p * 128 : (p + 1) * 128, :]
        sums = jnp.dot(part, pp[0], preferred_element_type=F32)
        sums = sums + jnp.dot(part, pp[1], preferred_element_type=F32)
        acc[p] = sums[0:32]
        for yo in range(1, NY):
            ys_buf[p, yo] = sums[yo * 32 : (yo + 1) * 32].astype(BF16)
        for yo in (2, 1, 3):
            send(ys_buf.at[p, yo], yr_buf.at[p, (NY - yo) % NY], "dense%d" % p, at(yo, 0, 0))
        if p == FAR_AFTER:
            arrived(f_in, "f_swap")
            theirs = f_in[...].astype(F32)
            far_all = halves(fown[...] + theirs + pltpu.roll(theirs, 64, 1))
            fs_buf[...] = far_all
            fr_buf[MID * 16 : (MID + 1) * 16, :] = far_all[MID * 16 : (MID + 1) * 16, :]
            for zo in Z_ORDER:
                slot, there = (MID + zo) % NZ, (MID - zo) % NZ
                send(fs_buf.at[pl.ds(slot * 16, 16)], fr_buf.at[pl.ds(there * 16, 16)], "z_far", at(0, zo, 0))


    for p in range(PARTS):
        arrived(yr_buf.at[p, pl.ds(1, 3)], "dense%d" % p)
        total = acc[p]
        for yo in range(1, NY):
            total = total + yr_buf[p, yo].astype(F32)
        total = total.astype(BF16)
        zs_buf[p * 32 : (p + 1) * 32, :] = total
        for i in range(2):
            zo = TO_Z[p * 2 + i]
            if zo == 0:
                zr_buf[(p * 2 + i) * 16 : (p * 2 + i + 1) * 16, :] = total[i * 16 : (i + 1) * 16]
            else:
                there = TO_Z.index(NZ - zo)
                send(
                    zs_buf.at[pl.ds((p * 2 + i) * 16, 16)], zr_buf.at[pl.ds(there * 16, 16)],
                    "z_near%d" % (there // 4), at(0, zo, 0),
                )
    left(x_tiles(0, 254), "y_own")
    left(coup.at[pl.ds(0, 6)], "coup")
    left(fg.at[pl.ds(0, 384)], "far")
    left(f_out, "f_swap")
    left(fs_buf.at[pl.ds(0, 240)], "z_far")
    left(pp.at[:, pl.ds(0, ROWS)], "pair")
    left(ys_buf.at[:, pl.ds(1, 3)], "dense0")
    local[8].wait()
    arrived(fr_buf.at[pl.ds(0, 240)], "z_far")
    far = fr_buf[0:16, :].astype(F32)
    for slot in range(1, NZ):
        far = far + fr_buf[slot * 16 : (slot + 1) * 16, :].astype(F32)
    far = (far + pltpu.roll(far, 64, 1)).astype(BF16).astype(F32)
    both = jnp.concatenate(
        [jnp.where(lane < 32, far, 0.0), jnp.where((lane >= 32) & (lane < 64), far, 0.0)], axis=0
    ).astype(BF16)
    basis = jnp.concatenate([tb[0], tb[1], jnp.zeros((64, 128), BF16)], axis=0)
    far = jnp.dot(both, basis, preferred_element_type=F32)
    near = zr_buf[240:256, :].astype(F32)
    for p in range(4):
        count = 4 if p < 3 else 3
        arrived(zr_buf.at[pl.ds(p * 64, count * 16)], "z_near%d" % p)
        for slot in range(p * 4, p * 4 + count):
            near = near + zr_buf[slot * 16 : (slot + 1) * 16, :].astype(F32)
    for u in range(2):
        for k in range(2):
            out[u * 8 : (u + 1) * 8, k * 128 : (k + 1) * 128] = (
                near[k * 8 : (k + 1) * 8, u * 128 : (u + 1) * 128]
                + far[k * 16 + u * 8 : k * 16 + (u + 1) * 8]
            )
    left(zs_buf.at[pl.ds(0, 240)], "z_near0")


def per_device(
    coeffs, near_blocks, near_scale, near_target, near_source, src_basis, tgt_basis, couplings, far_target, far_source
):
    dma = pltpu.SemaphoreType.DMA
    vmem, smem = pltpu.VMEM, pltpu.SMEM
    return pl.pallas_call(
        kernel,
        out_shape=jax.ShapeDtypeStruct((16, 256), F32),
        in_specs=[pl.BlockSpec(memory_space=pl.ANY)] * 10,
        out_specs=pl.BlockSpec(memory_space=pltpu.VMEM),
        scratch_shapes=[
            vmem((16, 256), BF16),
            vmem((BLK, 128, 128), BF16),
            smem((BLK,), jnp.int32),
            vmem((40, 128), jnp.int32),
            smem((5120,), jnp.int32),
            vmem((2, 32, 128), BF16),
            vmem((2, 32, 128), BF16),
            vmem((SHARE, 32, 32), BF16),
            vmem((PAIRS // 4, 32, 128), BF16),
            vmem((32, 128), jnp.int32),
            smem((4096,), jnp.int32),
            vmem((256, 16, 128), BF16),
            vmem((2, 2 * ROWS, 256), BF16),
            vmem((NY * 128, 256), BF16),
            vmem((2, 16, 128), BF16),
            vmem((16, 2 * ROWS), F32),
            vmem((2, 16, 128), F32),
            vmem((1024, 2 * ROWS), BF16),
            vmem((2, 512, 512), BF16),
            vmem((PARTS, 32, 256), F32),
            vmem((PARTS, NY, 32, 256), BF16),
            vmem((PARTS, NY, 32, 256), BF16),
            vmem((512, 256), F32),
            vmem((256, 128), F32),
            vmem((256, 128), BF16),
            vmem((256, 128), BF16),
            vmem((256, 256), BF16),
            vmem((256, 256), BF16),
            vmem((256, 128), BF16),
            vmem((256, 128), BF16),
            smem((BLK,), jnp.int32),
            dma((10,)),
            dma((len(RECV),)),
            dma((8,)),
        ],
        compiler_params=pltpu.CompilerParams(
            collective_id=0, has_side_effects=True, vmem_limit_bytes=60 * 1024 * 1024
        ),
        cost_estimate=pl.CostEstimate(flops=10**9, bytes_accessed=2 * 10**6, transcendentals=0),
        name="near_far_operator",
    )(
        coeffs, near_blocks, near_scale, near_target.reshape(40, 128), near_source, src_basis, tgt_basis,
        couplings, far_target.reshape(32, 128), far_source,
    )


def solution(mesh):
    placed = (
        P("rhs", "leaf"),
        P("leaf", None, None),
        P("leaf"),
        P(),
        P(),
        P("leaf", None, None),
        P("leaf", None, None),
        P(("leaf", "rhs"), None, None),
        P(),
        P(),
    )
    return jax.shard_map(
        per_device, mesh=mesh, in_specs=placed, out_specs=P("rhs", "leaf"), check_vma=False
    )
```

```python
import jax
import jax.numpy as jnp
from jax import lax
from jax.experimental import pallas as pl
from jax.experimental.pallas import tpu as pltpu
from jax.sharding import PartitionSpec as P

MESH = pl.DeviceIdType.MESH
NY, NZ, NX = 4, 16, 4
MID = 8
NEAR = (0, 1, 15, 2, 14, 3, 13, 4, 12, 5, 11, 6, 10, 7, 9, 8)
BLK = 40
ROWS = BLK * 8
PAIRS = 32
SHARE = 8
SPLITS = (0, 16, 32, BLK)
CLOSE = 3
LINES = ((CLOSE, 9 - CLOSE), (9, 7))
Z_ORDER = (8, 7, 9, 6, 10, 5, 11, 4, 12, 3, 13, 2, 14, 1, 15)
TO_Z = Z_ORDER + (0,)
FAR_AFTER = 1
DIRECT = (4, 12, 3, 13, 2, 14, 1, 15)
PARTS = 8
PLACE = (0, 1, 3, 2)
RECV_NAMES = (
    "y_own", "z_own", "z_close", "z_line", "y_line10", "y_line20", "y_line30", "y_line11", "y_line21", "y_line31", "core", "coup", "far", "f_swap", "pair",
    "dense0", "dense1", "dense2", "dense3", "dense4", "dense5", "dense6", "dense7",
    "z_far", "z_near0", "z_near1", "z_near2", "z_near3",
)
RECV = {name: i for i, name in enumerate(RECV_NAMES)}
SEND = dict(zip(RECV_NAMES, (0, 0, 0, 0, 0, 0, 0, 0, 0, 0, 0, 1, 2, 3, 4, 5, 5, 5, 5, 5, 5, 5, 5, 6, 7, 7, 7, 7)))
F32, BF16 = jnp.float32, jnp.bfloat16
NT = (((1,), (1,)), ((), ()))


def kernel(
    coeffs, blocks, scale, ntgt, nsrc, src_basis, tgt_basis, couplings, ftgt, fsrc,
    out,
    x_in, blk, scale_s, ntgt_v, nsrc_s, sb, tb, cp_in, coup, ftgt_v, fsrc_s,
    xg, pp, fg, bx, t2n, t2f, kr, kf, acc, ys_buf, yr_buf, fa, fown, f_out, f_in,
    zs_buf, zr_buf, fs_buf, fr_buf,
    index_s, lsem, rsem, ssem,
):
    me = lax.axis_index("leaf")
    x = lax.axis_index("rhs")
    y, z, c = me // 32, (me // 2) % 16, me % 2

    def leaf(yo, zo, co):
        return (((y + yo) % NY) * NZ + (z + zo) % NZ) * 2 + (c + co) % 2

    def at(yo, zo, co):
        return {"leaf": leaf(yo, zo, co)}

    x_copy = pltpu.make_async_copy(coeffs, x_in, lsem.at[9])
    x_copy.start()
    barrier = pltpu.get_barrier_semaphore()
    for zo in DIRECT:
        pl.semaphore_signal(barrier, inc=1, device_id=at(0, zo, 0), device_id_type=MESH)
    for yo in (2, 1, 3):
        pl.semaphore_signal(barrier, inc=1, device_id=at(yo, 0, 0), device_id_type=MESH)
    pl.semaphore_signal(barrier, inc=1, device_id=at(0, 0, 1), device_id_type=MESH)
    for xo in range(1, NX):
        pl.semaphore_signal(barrier, inc=1, device_id={"rhs": (x + xo) % NX}, device_id_type=MESH)

    local = []
    pairs = (
        (couplings, cp_in), (src_basis, sb), (ntgt, ntgt_v), (ftgt, ftgt_v), (fsrc, fsrc_s),
        (nsrc, nsrc_s), (scale, scale_s), (blocks, blk), (tgt_basis, tb),
    )
    for i, (a, b) in enumerate(pairs):
        copy = pltpu.make_async_copy(a, b, lsem.at[i])
        copy.start()
        local.append(copy)

    def copy_of(src, dst, name, device):
        return pltpu.make_async_remote_copy(
            src_ref=src, dst_ref=dst, send_sem=ssem.at[SEND[name]], recv_sem=rsem.at[RECV[name]],
            device_id=device, device_id_type=MESH,
        )

    def send(src, dst, name, device):
        copy_of(src, dst, name, device).start()

    def arrived(ref, name):
        copy_of(ref, ref, name, at(0, 0, 1)).wait_recv()

    def left(ref, name):
        copy_of(ref, ref, name, at(0, 0, 1)).wait_send()

    def x_tiles(first, count):
        return xg.at[pl.ds(first, count)]

    def close_at(slot, yo):
        return (slot * NY + yo) * 2

    def wide_at(slot, yo):
        return (CLOSE * NY + yo * (NZ - CLOSE) + slot - CLOSE) * 2

    def line_of(core, yo, group):
        first, count = LINES[group]
        return x_tiles(core * 128 + wide_at(first, yo), count * 2)

    x_copy.wait()
    xg[0] = x_in[:, 0:128]
    xg[1] = x_in[:, 128:256]
    pl.semaphore_wait(barrier, 15)

    own = x_tiles(0, 2)
    def piece(zo):
        slot = NEAR.index(zo % NZ)
        return x_tiles(close_at(slot, 0) if slot < CLOSE else wide_at(slot, 0), 2)

    for zo in DIRECT:
        send(own, piece(-zo), "z_own", at(0, zo, 0))

    for yo in (2, 1, 3):
        send(own, x_tiles(close_at(0, (NY - yo) % NY), 2), "y_own", at(yo, 0, 0))

    local[0].wait()
    i32 = lax.broadcasted_iota(jnp.int32, (32, 128), 0)
    lane32 = lax.broadcasted_iota(jnp.int32, (32, 128), 1)
    for t in range(SHARE // 4):
        packed = None
        for u in range(4):
            place = jnp.where(lane32 == i32 + u * 32, 1.0, 0.0).astype(BF16)
            part = jnp.dot(cp_in[t * 4 + u], place, preferred_element_type=F32)
            packed = part if packed is None else packed + part
        coup[x * (SHARE // 4) + t] = packed.astype(BF16)
    mine = coup.at[pl.ds(x * (SHARE // 4), SHARE // 4)]
    for xo in range(1, NX):
        send(mine, mine, "coup", {"rhs": (x + xo) % NX})

    local[1].wait()
    for k in range(2):
        four = jnp.concatenate([sb[k]] * 4, axis=0)
        part = lax.dot_general(xg[k], four, NT, preferred_element_type=F32)
        bx[k] = part.astype(BF16)

    local[2].wait()
    local[3].wait()
    lane = lax.broadcasted_iota(jnp.int32, (16, 128), 1)
    sub = lax.broadcasted_iota(jnp.int32, (16, 128), 0)
    first = (me // 2) * 2 * BLK
    row, off = first // 128, first % 128
    after = jnp.minimum(row + 1, BLK - 1)
    one = jnp.broadcast_to(ntgt_v[pl.ds(row, 1), :], (16, 128))
    two = jnp.broadcast_to(ntgt_v[pl.ds(after, 1), :], (16, 128))
    near_rows = pltpu.roll(jnp.where(lane >= off, one, two), (128 - off) % 128, 1)
    far_rows = jnp.zeros((16, 128), jnp.int32)
    for yo in range(NY):
        leaf_h = leaf(yo, 0, 0)
        frow, foff = leaf_h // 4, (leaf_h % 4) * 32
        fone = jnp.broadcast_to(ftgt_v[pl.ds(frow, 1), :], (16, 128))
        far_rows = jnp.where(sub == PLACE[yo], pltpu.roll(fone, (128 - foff) % 128, 1), far_rows)
    near_rows = near_rows.astype(F32).astype(BF16)
    far_rows = far_rows.astype(F32).astype(BF16)

    def spread(rows, width, step, start):
        b = lax.broadcasted_iota(jnp.int32, (128, width), 0)
        l = lax.broadcasted_iota(jnp.int32, (128, width), 1)
        pick = jnp.where(b == (l // 8) * step + start, 1.0, 0.0).astype(BF16)
        f = lax.broadcasted_iota(jnp.int32, (16, width), 1) % 8
        return jnp.dot(rows, pick, preferred_element_type=F32) * 8.0 + f.astype(F32)

    t2n[...] = spread(near_rows, 2 * ROWS, 1, 0)
    t2f[0] = spread(far_rows, 128, 2, 0)
    t2f[1] = spread(far_rows, 128, 2, 1)
    in_16 = sub.astype(F32)

    def ones(row, leaf_to):
        return jnp.where(row == in_16 + leaf_to * 16.0, 1.0, 0.0).astype(BF16)

    far_lanes = [[jnp.broadcast_to(t2f[g, h : h + 1, :], (16, 128)) for h in range(NY)] for g in range(2)]

    def build_far(i, carry):
        for part in range(2):
            rows = pl.ds(pl.multiple_of(part * 256 + i * 16, 16), 16)
            leaf_to = ((y * NZ + (z + i + NZ - MID) % NZ) * 2 + (c + part) % 2).astype(F32)
            for g in range(2):
                for h in range(NY):
                    kf[g, rows, h * 128 : (h + 1) * 128] = ones(far_lanes[g][h], leaf_to)
        return carry

    near_lanes = [jnp.broadcast_to(t2n[0:1, g * 128 : (g + 1) * 128], (16, 128)) for g in range(2 * ROWS // 128)]

    def build_near(i, carry):
        p, yo = i // NY, i % NY
        for slot in range(2):
            zo = MID + p if slot == 0 else MID - 1 - p
            rows = pl.ds(pl.multiple_of(i * 32 + slot * 16, 16), 16)
            leaf_to = ((((y + yo) % NY) * NZ + (z + zo) % NZ) * 2 + c).astype(F32)
            for g, row in enumerate(near_lanes):
                kr[rows, g * 128 : (g + 1) * 128] = ones(row, leaf_to)
        return carry

    lax.fori_loop(0, 16, build_far, 0)
    lax.fori_loop(0, PARTS * NY, build_near, 0)

    arrived(x_tiles(8, 16), "z_own")
    for zo in (4, 3, 13, 2, 14, 1, 15):
        far = zo + 4 if zo < MID else zo - 4
        send(piece(zo), piece(far), "z_line", at(0, zo - far, 0))
    def line_out(group):
        line = line_of(0, 0, group)
        for yo in (2, 1, 3):
            there = (NY - yo) % NY
            send(line, line_of(0, there, group), "y_line%d%d" % (there, group), at(yo, 0, 0))
        send(line, line_of(1, 0, group), "core", at(0, 0, 1))

    line_out(0)

    def close_forward():
        arrived(x_tiles(2, 6), "y_own")
        for zo in Z_ORDER[16 - CLOSE :]:
            slot = NEAR.index((NZ - zo) % NZ)
            send(x_tiles(2, 6), x_tiles(close_at(slot, 1), 6), "z_close", at(0, zo, 0))

    pl.when(c == 0)(close_forward)
    for i in (4, 5, 6):
        local[i].wait()
    arrived(coup.at[pl.ds(0, 6)], "coup")
    low_half = (lane // 32) % 2 == 1
    none = jnp.zeros((32, 128), BF16)
    for j in range(0, PAIRS // 2, 2):
        two = []
        for jj in (j, j + 1):
            total = None
            for g in range(2):
                q = 2 * jj + g
                mat = coup[q // 4]
                stack = [mat, mat, none, none] if g == 0 else [none, none, mat, mat]
                basis = bx[fsrc_s[me * PAIRS + q] % 2]
                basis = jnp.where(lane // 32 == q % 4, basis, jnp.zeros_like(basis))
                part = lax.dot_general(basis, jnp.concatenate(stack, axis=0), NT, preferred_element_type=F32)
                total = part if total is None else total + part
            high = total.astype(BF16).astype(F32)
            two.append(jnp.where(low_half, total - high, high))
        for u in range(2):
            half = jnp.concatenate([t[u * 8 : (u + 1) * 8] for t in two], axis=0)
            fg[j * 8 : (j + 2) * 8, u * 128 : (u + 1) * 128] = half.astype(BF16)

    for yo in (2, 1, 3):
        there = PLACE[(NY - yo) % NY]
        send(fg.at[pl.ds(0, 128)], fg.at[pl.ds(there * 128, 128)], "far", at(yo, 0, 0))

    def find(bb, carry):
        s = nsrc_s[me * BLK + bb]
        s_leaf = s // 2
        yo = (s_leaf // 32 + NY - y) % NY
        zo = ((s_leaf // 2) % 16 + NZ - z) % NZ
        zo = jnp.where(zo == 0, 0, jnp.where(zo <= 8, 2 * zo - 1, 2 * (NZ - zo)))
        co = (s_leaf + c) % 2
        tile = jnp.where(zo < CLOSE, zo * NY + yo, CLOSE * NY + yo * (NZ - CLOSE) + zo - CLOSE)
        index_s[bb] = co * 128 + tile * 2 + s % 2
        return carry

    lax.fori_loop(0, BLK, find, 0)
    arrived(x_tiles(wide_at(9, 0), 14), "z_line")
    line_out(1)
    pl.when(c == 1)(close_forward)
    arrived(x_tiles(8, (CLOSE - 1) * 6), "z_close")
    send(x_tiles(0, CLOSE * 8), x_tiles(128, CLOSE * 8), "core", at(0, 0, 1))

    def halves(v):
        high = v.astype(BF16).astype(F32)
        return jnp.where(lax.broadcasted_iota(jnp.int32, v.shape, 1) < 64, high, v - high).astype(BF16)

    arrived(fg.at[pl.ds(0, 384)], "far")
    first_pair = lax.broadcasted_iota(jnp.int32, (512, 256), 1) % 128 < 64
    terms = fg[...]
    zero = jnp.zeros_like(terms)
    fa[...] = jnp.dot(kf[0], jnp.where(first_pair, terms, zero), preferred_element_type=F32)
    fa[...] += jnp.dot(kf[1], jnp.where(first_pair, zero, terms), preferred_element_type=F32)
    even = (lane[0:8] // 32) % 2 == 0
    for part in (1, 0):
        for zs in range(NZ):
            columns = []
            for u in range(2):
                s = fa[part * 256 + zs * 16 : part * 256 + (zs + 1) * 16, u * 128 : (u + 1) * 128]
                s = s + pltpu.roll(s, 64, 1)
                s = s + pltpu.roll(s, 32, 1)
                columns.append(jnp.where(even, s[0:8], s[8:16]))
            v = jnp.concatenate(columns, axis=0)
            if part == 1:
                f_out[zs * 16 : (zs + 1) * 16, :] = halves(v)
            else:
                fown[zs * 16 : (zs + 1) * 16, :] = v
        if part == 1:
            send(f_out, f_in, "f_swap", at(0, 0, 1))

    for group in range(2):
        for yo in (1, 3, 2):
            line = line_of(0, yo, group)
            arrived(line, "y_line%d%d" % (yo, group))
            send(line, line_of(1, yo, group), "core", at(0, 0, 1))
    arrived(x_tiles(128, 128), "core")

    def share(first, count):
        rows = pl.ds(pl.multiple_of(c * ROWS + first * 8, 16), count * 8)
        send(pp.at[:, rows], pp.at[:, rows], "pair", at(0, 0, 1))

    local[7].wait()
    for b in range(0, BLK, 2):
        two = []
        for bb in (b, b + 1):
            index = index_s[bb]
            term = lax.dot_general(xg[index], blk[bb], NT, preferred_element_type=F32)
            two.append(term * jnp.exp2(jnp.full((16, 128), scale_s[bb], jnp.int32).astype(F32)))
        rows = pl.ds(pl.multiple_of(c * ROWS + b * 8, 16), 16)
        for u in range(2):
            half = jnp.concatenate([t[u * 8 : (u + 1) * 8] for t in two], axis=0)
            high = half.astype(BF16)
            pp[0, rows, u * 128 : (u + 1) * 128] = high
            pp[1, rows, u * 128 : (u + 1) * 128] = (half - high.astype(F32)).astype(BF16)
        if b + 2 in SPLITS:
            first = SPLITS[SPLITS.index(b + 2) - 1]
            share(first, b + 2 - first)

    arrived(pp.at[:, pl.ds(0, ROWS)], "pair")
    for p in range(PARTS):
        part = kr[p * 128 : (p + 1) * 128, :]
        sums = jnp.dot(part, pp[0], preferred_element_type=F32)
        sums = sums + jnp.dot(part, pp[1], preferred_element_type=F32)
        acc[p] = sums[0:32]
        for yo in range(1, NY):
            ys_buf[p, yo] = sums[yo * 32 : (yo + 1) * 32].astype(BF16)
        for yo in (2, 1, 3):
            send(ys_buf.at[p, yo], yr_buf.at[p, (NY - yo) % NY], "dense%d" % p, at(yo, 0, 0))
        if p == FAR_AFTER:
            arrived(f_in, "f_swap")
            theirs = f_in[...].astype(F32)
            far_all = halves(fown[...] + theirs + pltpu.roll(theirs, 64, 1))
            fs_buf[...] = far_all
            fr_buf[MID * 16 : (MID + 1) * 16, :] = far_all[MID * 16 : (MID + 1) * 16, :]
            for zo in Z_ORDER:
                slot, there = (MID + zo) % NZ, (MID - zo) % NZ
                send(fs_buf.at[pl.ds(slot * 16, 16)], fr_buf.at[pl.ds(there * 16, 16)], "z_far", at(0, zo, 0))


    for p in range(PARTS):
        arrived(yr_buf.at[p, pl.ds(1, 3)], "dense%d" % p)
        total = acc[p]
        for yo in range(1, NY):
            total = total + yr_buf[p, yo].astype(F32)
        total = total.astype(BF16)
        zs_buf[p * 32 : (p + 1) * 32, :] = total
        for i in range(2):
            zo = TO_Z[p * 2 + i]
            if zo == 0:
                zr_buf[(p * 2 + i) * 16 : (p * 2 + i + 1) * 16, :] = total[i * 16 : (i + 1) * 16]
            else:
                there = TO_Z.index(NZ - zo)
                send(
                    zs_buf.at[pl.ds((p * 2 + i) * 16, 16)], zr_buf.at[pl.ds(there * 16, 16)],
                    "z_near%d" % (there // 4), at(0, zo, 0),
                )
    left(x_tiles(0, 254), "y_own")
    left(coup.at[pl.ds(0, 6)], "coup")
    left(fg.at[pl.ds(0, 384)], "far")
    left(f_out, "f_swap")
    left(fs_buf.at[pl.ds(0, 240)], "z_far")
    left(pp.at[:, pl.ds(0, ROWS)], "pair")
    left(ys_buf.at[:, pl.ds(1, 3)], "dense0")
    local[8].wait()
    arrived(fr_buf.at[pl.ds(0, 240)], "z_far")
    far = fr_buf[0:16, :].astype(F32)
    for slot in range(1, NZ):
        far = far + fr_buf[slot * 16 : (slot + 1) * 16, :].astype(F32)
    far = (far + pltpu.roll(far, 64, 1)).astype(BF16).astype(F32)
    both = jnp.concatenate(
        [jnp.where(lane < 32, far, 0.0), jnp.where((lane >= 32) & (lane < 64), far, 0.0)], axis=0
    ).astype(BF16)
    basis = jnp.concatenate([tb[0], tb[1], jnp.zeros((64, 128), BF16)], axis=0)
    far = jnp.dot(both, basis, preferred_element_type=F32)
    near = zr_buf[240:256, :].astype(F32)
    for p in range(4):
        count = 4 if p < 3 else 3
        arrived(zr_buf.at[pl.ds(p * 64, count * 16)], "z_near%d" % p)
        for slot in range(p * 4, p * 4 + count):
            near = near + zr_buf[slot * 16 : (slot + 1) * 16, :].astype(F32)
    for u in range(2):
        for k in range(2):
            out[u * 8 : (u + 1) * 8, k * 128 : (k + 1) * 128] = (
                near[k * 8 : (k + 1) * 8, u * 128 : (u + 1) * 128]
                + far[k * 16 + u * 8 : k * 16 + (u + 1) * 8]
            )
    left(zs_buf.at[pl.ds(0, 240)], "z_near0")


def per_device(
    coeffs, near_blocks, near_scale, near_target, near_source, src_basis, tgt_basis, couplings, far_target, far_source
):
    dma = pltpu.SemaphoreType.DMA
    vmem, smem = pltpu.VMEM, pltpu.SMEM
    return pl.pallas_call(
        kernel,
        out_shape=jax.ShapeDtypeStruct((16, 256), F32),
        in_specs=[pl.BlockSpec(memory_space=pl.ANY)] * 10,
        out_specs=pl.BlockSpec(memory_space=pltpu.VMEM),
        scratch_shapes=[
            vmem((16, 256), BF16),
            vmem((BLK, 128, 128), BF16),
            smem((BLK,), jnp.int32),
            vmem((40, 128), jnp.int32),
            smem((5120,), jnp.int32),
            vmem((2, 32, 128), BF16),
            vmem((2, 32, 128), BF16),
            vmem((SHARE, 32, 32), BF16),
            vmem((PAIRS // 4, 32, 128), BF16),
            vmem((32, 128), jnp.int32),
            smem((4096,), jnp.int32),
            vmem((256, 16, 128), BF16),
            vmem((2, 2 * ROWS, 256), BF16),
            vmem((NY * 128, 256), BF16),
            vmem((2, 16, 128), BF16),
            vmem((16, 2 * ROWS), F32),
            vmem((2, 16, 128), F32),
            vmem((1024, 2 * ROWS), BF16),
            vmem((2, 512, 512), BF16),
            vmem((PARTS, 32, 256), F32),
            vmem((PARTS, NY, 32, 256), BF16),
            vmem((PARTS, NY, 32, 256), BF16),
            vmem((512, 256), F32),
            vmem((256, 128), F32),
            vmem((256, 128), BF16),
            vmem((256, 128), BF16),
            vmem((256, 256), BF16),
            vmem((256, 256), BF16),
            vmem((256, 128), BF16),
            vmem((256, 128), BF16),
            smem((BLK,), jnp.int32),
            dma((10,)),
            dma((len(RECV),)),
            dma((8,)),
        ],
        compiler_params=pltpu.CompilerParams(
            collective_id=0, has_side_effects=True, vmem_limit_bytes=60 * 1024 * 1024
        ),
        cost_estimate=pl.CostEstimate(flops=10**9, bytes_accessed=2 * 10**6, transcendentals=0),
        name="near_far_operator",
    )(
        coeffs, near_blocks, near_scale, near_target.reshape(40, 128), near_source, src_basis, tgt_basis,
        couplings, far_target.reshape(32, 128), far_source,
    )


def solution(mesh):
    placed = (
        P("rhs", "leaf"),
        P("leaf", None, None),
        P("leaf"),
        P(),
        P(),
        P("leaf", None, None),
        P("leaf", None, None),
        P(("leaf", "rhs"), None, None),
        P(),
        P(),
    )
    return jax.shard_map(
        per_device, mesh=mesh, in_specs=placed, out_specs=P("rhs", "leaf"), check_vma=False
    )
```
